128 devices in a mesh: slab: 4 (over y_hi, core), filt: 32 (over x, y_lo, z).
Axes of the slice: x: 4, y: 4 (y_hi: 2, y_lo: 2; y = y_hi * 2 + y_lo), z: 4, core: 2. Of those that a mesh axis runs over, the one named last changes fastest.
Arguments:
- volume: float32 [512, 32, 256], P('filt', 'slab'), may hold values from -6 to 6
- filters: float32 [27, 512, 512], P(None, 'filt'), may hold values from -0.0546875 to 0.0546875
- out_grad: float32 [512, 32, 256], P('filt', 'slab'), may hold values from -6 to 6
Outputs:
- activated: float32 [512, 32, 256], P('filt', 'slab')
- input_grad: float32 [512, 32, 256], P('filt', 'slab')
- weight_grad: float32 [27, 512, 512], P(None, 'filt')
The draws below stay inside these ranges and needn't reach their ends.
All inputs are finite; a program needn't handle non-finite values.
Results may differ from the reference program's by a relative error of at most 0.00012.
Values sent between devices are 32-bit elements; how exact they have to be, the bound alone decides.
A program may use at most 64 MiB of HBM per device.

```python
import jax
import jax.numpy as jnp
from jax import lax

C = 512
TAPS = 27
HEIGHT = 16
WIDTH = 16
DEPTH = 32


def level_of(key, shape, cuts, smallest, largest):
    def one(axis_at, parts):
        steps = jax.random.uniform(jax.random.fold_in(jax.random.fold_in(key, 6), axis_at), (parts,), jnp.float32, smallest / len(cuts), largest / len(cuts))
        return jnp.repeat(jnp.exp(steps), shape[axis_at] // parts).reshape((-1,) + (1,) * (len(shape) - axis_at - 1))

    factor_of = one(*cuts[0])
    for cut in cuts[1:]:
        factor_of = factor_of * one(*cut)
    return factor_of


def noise(key, extent, spread, limit, cuts=(), held_as=jnp.bfloat16):
    gain = level_of(key, extent, cuts, -0.22, 0.18) if cuts else 1.0
    entries = jax.random.normal(key, extent, jnp.float32) * spread * gain
    return jnp.minimum(jnp.maximum(entries, -limit), limit).astype(held_as)


def setup_inputs(seed: int = 0) -> dict:
    arg_keys = jax.random.split(jax.random.key(seed), 4)
    return {
        "volume": noise(arg_keys[0], (C, DEPTH, HEIGHT * WIDTH), 1.0, 6.0, ((0, 32), (1, 4)), jnp.float32),
        "filters": noise(arg_keys[1], (TAPS, C, C), (TAPS * C) ** -0.5, 0.0546875, ((1, 32),), jnp.float32),
        "out_grad": noise(arg_keys[2], (C, DEPTH, HEIGHT * WIDTH), 1.0, 6.0, ((0, 32), (1, 4)), jnp.float32),
    }


def convolve(inputs, kernel):
    return lax.conv_general_dilated(inputs, kernel, (1, 1, 1), [(1, 1), (1, 1), (1, 1)], dimension_numbers=('NCDHW', 'OIDHW', 'NCDHW'), precision=lax.Precision.HIGHEST)

def reference(volume, filters, out_grad):
    inputs = volume.reshape(1, C, DEPTH, HEIGHT, WIDTH)
    kernel = filters.reshape(3, 3, 3, C, C).transpose(3, 4, 0, 1, 2)
    preact, pullback = jax.vjp(convolve, inputs, kernel)
    positive = jnp.maximum(preact, 0.0)
    activated = positive * positive
    pre_grad = 2.0 * positive * out_grad.reshape(preact.shape)
    grad_inputs, grad_kernel = pullback(pre_grad)
    voxels = DEPTH * HEIGHT * WIDTH
    weight_grad = grad_kernel.transpose(2, 3, 4, 0, 1).reshape(TAPS, C, C) / jnp.sqrt(jnp.float32(voxels))
    return (activated.reshape(C, DEPTH, HEIGHT * WIDTH), grad_inputs.reshape(C, DEPTH, HEIGHT * WIDTH), weight_grad)
```

```python
import math

import jax
import jax.numpy as jnp
from jax import lax
from jax.experimental import pallas as pl
from jax.experimental.pallas import tpu as pltpu
from jax.sharding import PartitionSpec as P

TAPS = 27
PAD = 28
WIDTH = 16
PLANE = 256
ROWS = 16
PLANES = 8
SLABS = 4
X, GY, GZ = 4, 2, 4

GATHER_CHUNKS = ((0, 2), (6, 2), (2, 2), (4, 2))
REDUCE_CHUNKS = ((0, 2), (2, 2), (4, 2), (6, 2))
INPUT_CHUNKS = ((2, 2), (4, 2), (0, 2), (6, 2))

F32 = jnp.float32
BF16 = jnp.bfloat16


def split(value):
    high = value.astype(BF16)
    low = (value - high.astype(F32)).astype(BF16)
    return high, low


def product(left_high, left_low, right_high, right_low, dims):
    def one(left, right):
        return lax.dot_general(left, right, (dims, ((), ())), preferred_element_type=F32)

    return one(left_high, right_high) + (one(left_high, right_low) + one(left_low, right_high))


def kernel(
    vol, fil, og, act, ig, wg,
    g32, gh, gl, fa, w9h, w9l, wc, wth, wtl, taps, part, prec, pgx, sh, sl,
    wacc, wsum, w1b, w2b, wout, igp, igr,
    gat_s, gat_r, fil_s, fil_r, hal_s, hal_r, rs_s, rs_r, ag_s, ag_r, ph_s, ph_r,
    in_s, in_r, w1_s, w1_r, w2_s, w2_r, w3_s, w3_r, w5_s, w5_r,
):
    G = GY * GZ
    I = ROWS * G
    O = ROWS * X
    s = lax.axis_index("slab")
    f = lax.axis_index("filt")
    x = f // G
    g = f % G
    gy = g // GZ
    gz = g % GZ
    core = s % 2
    half = s // 2
    mate = half * 2 + (1 - core)
    across = (s + 2) % SLABS
    other = (mate + 2) % SLABS

    def along_x(j):
        return (x + j) % X

    group = []
    for dy in range(GY):
        for dz in range(GZ):
            if dy or dz:
                group.append(((gy + dy) % GY) * GZ + (gz + dz) % GZ)

    def rows(index):
        return pl.ds(pl.multiple_of(index * ROWS, ROWS), ROWS)

    barrier = pltpu.get_barrier_semaphore()
    partners = [(s, x * G + to) for to in group]
    partners += [(s, along_x(j) * G + g) for j in range(1, X)]
    partners += [(across, along_x(j) * G + g) for j in range(1, X)]
    partners += [(mate, f), (across, f), (other, f)]
    for partner in partners:
        pl.semaphore_signal(
            barrier, inc=1, device_id=partner, device_id_type=pl.DeviceIdType.MESH
        )

    for d in range(PLANES):
        g32[1 + d, rows(g), :] = vol[:, d, :]

    pl.semaphore_wait(barrier, len(partners))

    def remote(src, dst, send, recv, device):
        return pltpu.make_async_remote_copy(
            src_ref=src, dst_ref=dst, send_sem=send, recv_sem=recv,
            device_id=device, device_id_type=pl.DeviceIdType.MESH,
        )

    sent = []

    gather = {}
    for n, (d, w) in enumerate(GATHER_CHUNKS):
        for j, to in enumerate(group):
            here = g32.at[pl.ds(1 + d, w), rows(g), :]
            copy = remote(here, here, gat_s.at[n, j], gat_r.at[n, j], (s, x * G + to))
            copy.start()
            gather.setdefault(n, []).append(copy)
            sent.append(copy)
    filters = []
    for j in range(1, X):
        to = along_x(j)
        copy = remote(
            fil.at[:, :, pl.ds(pl.multiple_of(to * I, I), I)], fa.at[x],
            fil_s.at[j - 1], fil_r.at[j - 1], (s, to * G + g),
        )
        copy.start()
        filters.append(copy)
        sent.append(copy)
    fa[x] = fil[:, :, pl.ds(pl.multiple_of(x * I, I), I)]

    @pl.when(s == 0)
    def _():
        g32[0] = jnp.zeros((I, PLANE), F32)
        pgx[0] = jnp.zeros((O, PLANE), F32)

    @pl.when(s == SLABS - 1)
    def _():
        g32[PLANES + 1] = jnp.zeros((I, PLANE), F32)
        pgx[PLANES + 1] = jnp.zeros((O, PLANE), F32)

    wsum[:, TAPS] = jnp.zeros((X, ROWS, I), F32)
    wc[TAPS * O :] = jnp.zeros((wc.shape[0] - TAPS * O, I), F32)

    for copy in filters:
        copy.wait_recv()
    for a in range(3):
        for k in range(9):
            block = fa[:, 9 * a + k].reshape(O, I)
            high, low = split(block)
            w9h[k * O : (k + 1) * O, a * I : (a + 1) * I] = high
            w9l[k * O : (k + 1) * O, a * I : (a + 1) * I] = low
            wc[((2 - a) * 9 + k) * O : ((2 - a) * 9 + k + 1) * O, :] = block

    def transpose(n, carry):
        start = pl.multiple_of(n * 128, 128)
        high, low = split(wc[pl.ds(start, 128), :].T)
        wth[:, pl.ds(start, 128)] = high
        wtl[:, pl.ds(start, 128)] = low
        return carry

    lax.fori_loop(0, wc.shape[0] // 128, transpose, 0)

    def neighbours(buffer, send, recv):
        up = remote(
            buffer.at[PLANES], buffer.at[0], send.at[0], recv.at[0], ((s + 1) % SLABS, f)
        )
        down = remote(
            buffer.at[1], buffer.at[PLANES + 1], send.at[1], recv.at[1], ((s + 3) % SLABS, f)
        )

        def start():
            @pl.when(s < SLABS - 1)
            def _():
                up.start()

            @pl.when(s > 0)
            def _():
                down.start()

        def arrive():
            @pl.when(s > 0)
            def _():
                up.wait_recv()

            @pl.when(s < SLABS - 1)
            def _():
                down.wait_recv()

        def leave():
            @pl.when(s < SLABS - 1)
            def _():
                up.wait_send()

            @pl.when(s > 0)
            def _():
                down.wait_send()

        return start, arrive, leave

    edge_start, edge_arrive, edge_leave = neighbours(g32, hal_s, hal_r)
    rim_start, rim_arrive, rim_leave = neighbours(pgx, ph_s, ph_r)

    def halve(e, carry):
        high, low = split(g32[e])
        gh[e] = high
        gl[e] = low
        return carry

    for n in range(len(GATHER_CHUNKS)):
        for copy in gather[n]:
            copy.wait_recv()
        if n == 1:
            edge_start()
    lax.fori_loop(1, PLANES + 1, halve, 0)
    edge_arrive()
    halve(0, 0)
    halve(PLANES + 1, 0)

    lane = lax.broadcasted_iota(jnp.int32, (O, PLANE), 1)
    column = lane % WIDTH
    not_left = column >= 1
    not_right = column <= WIDTH - 2
    not_top = lane >= WIDTH
    not_bottom = lane < PLANE - WIDTH

    def forward(d, carry):
        right_high = gh[pl.ds(d, 3)].reshape(3 * I, PLANE)
        right_low = gl[pl.ds(d, 3)].reshape(3 * I, PLANE)
        taps[...] = product(w9h[...], w9l[...], right_high, right_low, ((1,), (0,)))

        def line(b):
            def tap(c):
                k = 3 * b + c
                return taps[k * O : (k + 1) * O, :]

            total = tap(1)
            total += jnp.where(not_left, pltpu.roll(tap(0), 1, 1), 0.0)
            total += jnp.where(not_right, pltpu.roll(tap(2), PLANE - 1, 1), 0.0)
            return total

        total = line(1)
        total += jnp.where(not_top, pltpu.roll(line(0), WIDTH, 1), 0.0)
        total += jnp.where(not_bottom, pltpu.roll(line(2), PLANE - WIDTH, 1), 0.0)
        part[d] = total
        return carry

    reduce = []
    for n, (d, w) in enumerate(REDUCE_CHUNKS):
        lax.fori_loop(d, d + w, forward, 0)
        copies = []
        for j in range(1, X):
            to = along_x(j)
            copy = remote(
                part.at[pl.ds(d, w), rows(to), :], prec.at[j - 1, pl.ds(d, w)],
                rs_s.at[n, j - 1], rs_r.at[n, j - 1], (s, to * G + g),
            )
            copy.start()
            copies.append(copy)
            sent.append(copy)
        reduce.append(copies)

    spread = []
    for n, (d, w) in enumerate(REDUCE_CHUNKS):
        for copy in reduce[n]:
            copy.wait_recv()
        for e in range(d, d + w):
            total = part[e, rows(x), :]
            for j in range(X - 1):
                total += prec[j, e]
            positive = jnp.maximum(total, 0.0)
            act[:, e, :] = positive * positive
            pgx[1 + e, rows(x), :] = 2.0 * positive * og[:, e, :]
        copies = []
        for j in range(1, X):
            here = pgx.at[pl.ds(1 + d, w), rows(x), :]
            copy = remote(
                here, here, ag_s.at[n, j - 1], ag_r.at[n, j - 1], (s, along_x(j) * G + g)
            )
            copy.start()
            copies.append(copy)
            sent.append(copy)
        spread.append(copies)

    def stack(e, carry):
        field = pgx[e]
        for b in range(3):
            if b == 0:
                moved = jnp.where(not_bottom, pltpu.roll(field, PLANE - WIDTH, 1), 0.0)
            elif b == 1:
                moved = field
            else:
                moved = jnp.where(not_top, pltpu.roll(field, WIDTH, 1), 0.0)
            for c in range(3):
                if c == 0:
                    last = jnp.where(not_right, pltpu.roll(moved, PLANE - 1, 1), 0.0)
                elif c == 1:
                    last = moved
                else:
                    last = jnp.where(not_left, pltpu.roll(moved, 1, 1), 0.0)
                k = 3 * b + c
                high, low = split(last)
                sh[e, k * O : (k + 1) * O, :] = high
                sl[e, k * O : (k + 1) * O, :] = low
        return carry

    def weigh(d, carry):
        stack(d + 1, 0)
        term = product(
            sh[d + 1], sl[d + 1],
            gh[pl.ds(d, 3)].reshape(3 * I, PLANE), gl[pl.ds(d, 3)].reshape(3 * I, PLANE),
            ((1,), (1,)),
        )
        wacc[...] += term
        return carry

    wacc[...] = jnp.zeros_like(wacc)
    for n, (d, w) in enumerate(REDUCE_CHUNKS):
        for copy in spread[n]:
            copy.wait_recv()
        lax.fori_loop(d, d + w, weigh, 0)
    rim_start()

    for a in range(3):
        for k in range(9):
            block = wacc[k * O : (k + 1) * O, a * I : (a + 1) * I]
            wsum[:, 9 * a + k] = block.reshape(X, ROWS, I)

    H = PAD // 2
    Q = PAD // 4
    near = core * H
    quarter = near + half * Q
    first = remote(
        wsum.at[:, pl.ds((1 - core) * H, H)], w1b, w1_s, w1_r, (mate, f)
    )
    first.start()
    sent.append(first)

    def backward(d, carry):
        igp[d] = product(
            wth[:, : TAPS * O], wtl[:, : TAPS * O],
            sh[pl.ds(d, 3)].reshape(TAPS * O, PLANE), sl[pl.ds(d, 3)].reshape(TAPS * O, PLANE),
            ((1,), (0,)),
        )
        return carry

    inward = []

    def input_chunk(n):
        d, w = INPUT_CHUNKS[n]
        lax.fori_loop(d, d + w, backward, 0)
        copies = []
        for j, to in enumerate(group):
            copy = remote(
                igp.at[pl.ds(d, w), rows(to), :], igr.at[j, pl.ds(d, w)],
                in_s.at[n, j], in_r.at[n, j], (s, x * G + to),
            )
            copy.start()
            copies.append(copy)
            sent.append(copy)
        inward.append(copies)

    input_chunk(0)

    first.wait_recv()
    wsum[:, pl.ds(near, H)] += w1b[...]
    second = remote(
        wsum.at[:, pl.ds(near + (1 - half) * Q, Q)], w2b, w2_s, w2_r, (across, f)
    )
    second.start()
    sent.append(second)

    input_chunk(1)
    rim_arrive()
    stack(0, 0)
    stack(PLANES + 1, 0)
    input_chunk(2)

    scale = 1.0 / math.sqrt(PLANES * SLABS * PLANE)
    second.wait_recv()
    wsum[:, pl.ds(quarter, Q)] = (wsum[:, pl.ds(quarter, Q)] + w2b[...]) * scale
    third = []
    lanes = pl.ds(pl.multiple_of(x * I, I), I)
    for j in range(X):
        to = along_x(j)
        for k, slab in enumerate((s, across)):
            if j == 0 and k == 0:
                continue
            copy = remote(
                wsum.at[to, pl.ds(quarter, Q)], wout.at[pl.ds(quarter, Q), :, lanes],
                w3_s.at[j, k], w3_r.at[j, k], (slab, to * G + g),
            )
            copy.start()
            third.append(copy)
            sent.append(copy)
    wout[pl.ds(quarter, Q), :, lanes] = wsum[x, pl.ds(quarter, Q)]

    input_chunk(3)

    for copy in third:
        copy.wait_recv()
    here = wout.at[pl.ds(near, H)]
    last = remote(here, here, w5_s, w5_r, (mate, f))
    last.start()
    sent.append(last)

    for n, (d, w) in enumerate(INPUT_CHUNKS):
        for copy in inward[n]:
            copy.wait_recv()
        for e in range(d, d + w):
            total = igp[e, rows(g), :]
            for j in range(G - 1):
                total += igr[j, e]
            ig[:, e, :] = total

    last.wait_recv()
    wg[...] = wout[:TAPS]

    for copy in sent:
        copy.wait_send()
    edge_leave()
    rim_leave()


def scratch():
    G = GY * GZ
    I = ROWS * G
    O = ROWS * X
    columns = -(-TAPS * O // 128) * 128
    vmem = pltpu.VMEM
    dma = pltpu.SemaphoreType.DMA
    return [
        vmem((PLANES + 2, I, PLANE), F32),
        vmem((PLANES + 2, I, PLANE), BF16),
        vmem((PLANES + 2, I, PLANE), BF16),
        vmem((X, TAPS, ROWS, I), F32),
        vmem((9 * O, 3 * I), BF16),
        vmem((9 * O, 3 * I), BF16),
        vmem((columns, I), F32),
        vmem((I, columns), BF16),
        vmem((I, columns), BF16),
        vmem((9 * O, PLANE), F32),
        vmem((PLANES, O, PLANE), F32),
        vmem((X - 1, PLANES, ROWS, PLANE), F32),
        vmem((PLANES + 2, O, PLANE), F32),
        vmem((PLANES + 2, 9 * O, PLANE), BF16),
        vmem((PLANES + 2, 9 * O, PLANE), BF16),
        vmem((9 * O, 3 * I), F32),
        vmem((X, PAD, ROWS, I), F32),
        vmem((X, PAD // 2, ROWS, I), F32),
        vmem((X, PAD // 4, ROWS, I), F32),
        vmem((PAD, ROWS, X * I), F32),
        vmem((PLANES, I, PLANE), F32),
        vmem((G - 1, PLANES, ROWS, PLANE), F32),
        dma((len(GATHER_CHUNKS), G - 1)), dma((len(GATHER_CHUNKS), G - 1)),
        dma((X - 1,)), dma((X - 1,)),
        dma((2,)), dma((2,)),
        dma((len(REDUCE_CHUNKS), X - 1)), dma((len(REDUCE_CHUNKS), X - 1)),
        dma((len(REDUCE_CHUNKS), X - 1)), dma((len(REDUCE_CHUNKS), X - 1)),
        dma((2,)), dma((2,)),
        dma((len(INPUT_CHUNKS), G - 1)), dma((len(INPUT_CHUNKS), G - 1)),
        dma, dma, dma, dma,
        dma((X, 2)), dma((X, 2)),
        dma, dma,
    ]


def shards(volume, filters, out_grad):
    whole = pl.BlockSpec(memory_space=pltpu.VMEM)
    return pl.pallas_call(
        kernel,
        out_shape=(
            jax.ShapeDtypeStruct(volume.shape, F32),
            jax.ShapeDtypeStruct(volume.shape, F32),
            jax.ShapeDtypeStruct(filters.shape, F32),
        ),
        in_specs=[whole] * 3,
        out_specs=(whole,) * 3,
        scratch_shapes=scratch(),
        compiler_params=pltpu.CompilerParams(
            collective_id=0, has_side_effects=True, vmem_limit_bytes=56 * 2**20
        ),
    )(volume, filters, out_grad)


def solution(mesh):
    placed = (P("filt", "slab", None), P(None, "filt", None), P("filt", "slab", None))
    return jax.shard_map(
        shards,
        mesh=mesh,
        in_specs=placed,
        out_specs=(P("filt", "slab", None), P("filt", "slab", None), P(None, "filt", None)),
        check_vma=False,
    )
```

```python
import math

import jax
import jax.numpy as jnp
from jax import lax
from jax.experimental import pallas as pl
from jax.experimental.pallas import tpu as pltpu
from jax.sharding import PartitionSpec as P

TAPS = 27
PAD = 28
WIDTH = 16
PLANE = 256
ROWS = 16
PLANES = 8
SLABS = 4
X, GY, GZ = 4, 2, 4
G = GY * GZ

GATHER_CHUNKS = ((0, 2, 1), (6, 2, -1), (2, 2, 1), (4, 2, -1))
REDUCE_CHUNKS = ((0, 2, 1), (2, 2, -1), (4, 2, 1), (6, 2, -1))
INPUT_CHUNKS = ((2, 2, 1), (4, 2, -1), (0, 2, 1), (6, 2, -1))
TAP_CHUNKS = ((0, 4, 1), (7, 4, -1), (4, 3, 1), (11, 3, -1))

F32 = jnp.float32
BF16 = jnp.bfloat16


def split(value):
    high = value.astype(BF16)
    low = (value - high.astype(F32)).astype(BF16)
    return high, low


def product(left_high, left_low, right_high, right_low, dims):
    def one(left, right):
        return lax.dot_general(left, right, (dims, ((), ())), preferred_element_type=F32)

    return one(left_high, right_high) + (one(left_high, right_low) + one(left_low, right_high))


def kernel(
    vol, fil, og, act, ig, wg,
    volv, ogv, actv, igv,
    g32, gh, gl, fa, w9h, w9l, wc, wth, wtl, taps, part, prec, pgx, sh, sl,
    wacc, wsum, w1b, wrel, warr, wtot, wout, igp, zrel, zrec, yrec,
    local, g_s, g_r, fil_s, fil_r, hal_s, hal_r, rs_s, rs_r, ag_s, ag_r, ph_s, ph_r,
    in_s, in_r, w1_s, w1_r, wy_s, wy_r, wx_s, wx_r, w5_s, w5_r,
):
    I = ROWS * G
    O = ROWS * X
    H = PAD // 2
    s = lax.axis_index("slab")
    f = lax.axis_index("filt")
    x = f // G
    g = f % G
    gy = g // GZ
    gz = g % GZ
    core = s % 2
    half = s // 2
    mate = half * 2 + (1 - core)
    across = (s + 2) % SLABS
    other = (mate + 2) % SLABS

    def x_of(j):
        return (x + j + X) % X

    def z_of(j):
        return (gz + j + GZ) % GZ

    def at_x(j):
        return (s, x_of(j) * G + g)

    def at_z(j):
        return (s, x * G + gy * GZ + z_of(j))

    flipped = x * G + (1 - gy) * GZ + gz
    at_y = (s, flipped)
    next_y = (((half + gy) % 2) * 2 + core, flipped)
    prev_y = (((half + 1 - gy) % 2) * 2 + core, flipped)

    def rows(index):
        return pl.ds(pl.multiple_of(index * ROWS, ROWS), ROWS)

    def lanes(index):
        return pl.ds(pl.multiple_of(index * I, I), I)

    barrier = pltpu.get_barrier_semaphore()
    partners = [
        (mate, f), at_y, at_z(1), at_z(-1), at_x(1), at_x(-1), at_x(2), (other, f),
        (across, flipped),
    ]
    for partner in partners:
        pl.semaphore_signal(
            barrier, inc=1, device_id=partner, device_id_type=pl.DeviceIdType.MESH
        )

    bring_vol = pltpu.make_async_copy(vol, volv, local.at[0])
    bring_og = pltpu.make_async_copy(og, ogv, local.at[1])
    bring_fil = pltpu.make_async_copy(fil.at[:, :, lanes(x)], fa.at[x], local.at[2])
    bring_vol.start()
    bring_og.start()
    bring_fil.start()

    @pl.when(s == 0)
    def _():
        g32[0] = jnp.zeros((GY, GZ * ROWS, PLANE), F32)
        pgx[0] = jnp.zeros((O, PLANE), F32)

    @pl.when(s == SLABS - 1)
    def _():
        g32[PLANES + 1] = jnp.zeros((GY, GZ * ROWS, PLANE), F32)
        pgx[PLANES + 1] = jnp.zeros((O, PLANE), F32)

    wsum[:, TAPS] = jnp.zeros((X, ROWS, I), F32)
    wc[TAPS * O :] = jnp.zeros((wc.shape[0] - TAPS * O, I), F32)
    wacc[...] = jnp.zeros_like(wacc)

    bring_vol.wait()
    for d in range(PLANES):
        g32[1 + d, gy, rows(gz), :] = volv[:, d, :]

    pl.semaphore_wait(barrier, len(partners))

    sent = []
    leaves = []

    def remote(src, dst, send, recv, device):
        return pltpu.make_async_remote_copy(
            src_ref=src, dst_ref=dst, send_sem=send, recv_sem=recv,
            device_id=device, device_id_type=pl.DeviceIdType.MESH,
        )

    def push(src, dst, sems, index, device):
        send, recv = sems
        copy = remote(src, dst, send.at[index], recv.at[index], device)
        copy.start()
        sent.append(copy)
        return copy


    strip = pl.ds(pl.multiple_of(core * (ROWS // 2), ROWS // 2), ROWS // 2)
    fil_sems = (fil_s, fil_r)
    filters = []
    for j in (1, 3, 2):
        filters.append(
            (
                x_of(-j),
                push(
                    fil.at[:, strip, lanes(x_of(j))], fa.at[x, :, strip], fil_sems, j - 1, at_x(j)
                ),
            )
        )
    g_sems = (g_s, g_r)
    gather = []
    for n, (d, w, way) in enumerate(GATHER_CHUNKS):
        here = g32.at[pl.ds(1 + d, w), gy, rows(gz), :]
        gather.append(
            {
                "y": push(here, here, g_sems, (n, 0), at_y),
                ("own", 1): push(here, here, g_sems, (n, 1), at_z(1)),
                ("own", -1): push(here, here, g_sems, (n, 2), at_z(-1)),
            }
        )
    for n, (d, w, way) in enumerate(GATHER_CHUNKS):
        gather[n]["y"].wait_recv()
        here = g32.at[pl.ds(1 + d, w), 1 - gy, rows(gz), :]
        gather[n]["pair", 1] = push(here, here, g_sems, (n, 3), at_z(1))
        gather[n]["pair", -1] = push(here, here, g_sems, (n, 4), at_z(-1))
    for n, (d, w, way) in enumerate(GATHER_CHUNKS):
        gather[n]["own", way].wait_recv()
        gather[n]["pair", way].wait_recv()
        here = g32.at[pl.ds(1 + d, w), :, rows(z_of(-way)), :]
        gather[n]["far"] = push(here, here, g_sems, (n, 5), at_z(way))

    swaps = []
    for n, (source, copy) in enumerate(filters):
        copy.wait_recv()
        here = fa.at[source, :, strip]
        swaps.append(push(here, here, fil_sems, 3 + n, (mate, f)))
    bring_fil.wait()
    for copy in swaps:
        copy.wait_recv()

    for a in range(3):
        for k in range(9):
            block = fa[:, 9 * a + k].reshape(O, I)
            high, low = split(block)
            w9h[k * O : (k + 1) * O, a * I : (a + 1) * I] = high
            w9l[k * O : (k + 1) * O, a * I : (a + 1) * I] = low
            wc[((2 - a) * 9 + k) * O : ((2 - a) * 9 + k + 1) * O, :] = block

    def transpose(n, carry):
        start = pl.multiple_of(n * 128, 128)
        high, low = split(wc[pl.ds(start, 128), :].T)
        wth[:, pl.ds(start, 128)] = high
        wtl[:, pl.ds(start, 128)] = low
        return carry

    def neighbours(buffer, send, recv):
        up = remote(
            buffer.at[PLANES], buffer.at[0], send.at[0], recv.at[0], ((s + 1) % SLABS, f)
        )
        down = remote(
            buffer.at[1], buffer.at[PLANES + 1], send.at[1], recv.at[1], ((s + 3) % SLABS, f)
        )

        def start():
            @pl.when(s < SLABS - 1)
            def _():
                up.start()

            @pl.when(s > 0)
            def _():
                down.start()

        def arrive():
            @pl.when(s > 0)
            def _():
                up.wait_recv()

            @pl.when(s < SLABS - 1)
            def _():
                down.wait_recv()

        def leave():
            @pl.when(s < SLABS - 1)
            def _():
                up.wait_send()

            @pl.when(s > 0)
            def _():
                down.wait_send()

        return start, arrive, leave

    edge_start, edge_arrive, edge_leave = neighbours(g32, hal_s, hal_r)

    def halve(e, carry):
        high, low = split(g32[e].reshape(I, PLANE))
        gh[e] = high
        gl[e] = low
        return carry

    for n, (d, w, way) in enumerate(GATHER_CHUNKS):
        gather[n]["own", -way].wait_recv()
        gather[n]["pair", -way].wait_recv()
        gather[n]["far"].wait_recv()
        if n == 1:
            edge_start()
            leaves.append(edge_leave)
    lax.fori_loop(1, PLANES + 1, halve, 0)

    lane = lax.broadcasted_iota(jnp.int32, (O, PLANE), 1)
    column = lane % WIDTH
    not_left = column >= 1
    not_right = column <= WIDTH - 2
    not_top = lane >= WIDTH
    not_bottom = lane < PLANE - WIDTH

    def forward(d, carry):
        right_high = gh[pl.ds(d, 3)].reshape(3 * I, PLANE)
        right_low = gl[pl.ds(d, 3)].reshape(3 * I, PLANE)
        taps[...] = product(w9h[...], w9l[...], right_high, right_low, ((1,), (0,)))

        def line(b):
            def tap(c):
                k = 3 * b + c
                return taps[k * O : (k + 1) * O, :]

            total = tap(1)
            total += jnp.where(not_left, pltpu.roll(tap(0), 1, 1), 0.0)
            total += jnp.where(not_right, pltpu.roll(tap(2), PLANE - 1, 1), 0.0)
            return total

        total = line(1)
        total += jnp.where(not_top, pltpu.roll(line(0), WIDTH, 1), 0.0)
        total += jnp.where(not_bottom, pltpu.roll(line(2), PLANE - WIDTH, 1), 0.0)
        part[d] = total
        return carry

    rs_sems = (rs_s, rs_r)
    reduce = []

    def reduce_start(n):
        d, w, way = REDUCE_CHUNKS[n]
        planes = pl.ds(d, w)
        reduce.append(
            [
                push(
                    part.at[planes, rows(x_of(j)), :], prec.at[j - 1, planes],
                    rs_sems, (n, j - 1), at_x(j),
                )
                for j in (2, 1, 3)
            ]
        )

    ag_sems = (ag_s, ag_r)
    spread = []

    def activate(n):
        d, w, way = REDUCE_CHUNKS[n]
        for copy in reduce[n]:
            copy.wait_recv()
        for e in range(d, d + w):
            total = part[e, rows(x), :] + prec[0, e] + (prec[1, e] + prec[2, e])
            positive = jnp.maximum(total, 0.0)
            actv[:, e, :] = positive * positive
            pgx[1 + e, rows(x), :] = 2.0 * positive * ogv[:, e, :]
        here = pgx.at[pl.ds(1 + d, w), rows(x), :]
        spread.append([push(here, here, ag_sems, (n, j - 1), at_x(j)) for j in (2, 1, 3)])

    edge_arrive()
    halve(0, 0)
    halve(PLANES + 1, 0)
    for n, (d, w, way) in enumerate(REDUCE_CHUNKS):
        lax.fori_loop(d, d + w, forward, 0)
        reduce_start(n)
        if n == 1:
            bring_og.wait()
        if n > 1:
            activate(n - 2)
    lax.fori_loop(0, wc.shape[0] // 128, transpose, 0)
    activate(2)
    activate(3)
    give_act = pltpu.make_async_copy(actv, act, local.at[0])
    give_act.start()

    def stack(e, carry):
        field = pgx[e]
        for b in range(3):
            if b == 0:
                moved = jnp.where(not_bottom, pltpu.roll(field, PLANE - WIDTH, 1), 0.0)
            elif b == 1:
                moved = field
            else:
                moved = jnp.where(not_top, pltpu.roll(field, WIDTH, 1), 0.0)
            for c in range(3):
                if c == 0:
                    last = jnp.where(not_right, pltpu.roll(moved, PLANE - 1, 1), 0.0)
                elif c == 1:
                    last = moved
                else:
                    last = jnp.where(not_left, pltpu.roll(moved, 1, 1), 0.0)
                k = 3 * b + c
                high, low = split(last)
                sh[e, k * O : (k + 1) * O, :] = high
                sl[e, k * O : (k + 1) * O, :] = low
        return carry

    def weigh(d, carry):
        stack(d + 1, 0)
        term = product(
            sh[d + 1], sl[d + 1],
            gh[pl.ds(d, 3)].reshape(3 * I, PLANE), gl[pl.ds(d, 3)].reshape(3 * I, PLANE),
            ((1,), (1,)),
        )
        wacc[...] += term
        return carry

    rim_start, rim_arrive, rim_leave = neighbours(pgx, ph_s, ph_r)
    for n, (d, w, way) in enumerate(REDUCE_CHUNKS):
        for copy in spread[n]:
            copy.wait_recv()
        if n == 3:
            rim_start()
            leaves.append(rim_leave)
        lax.fori_loop(d, d + w, weigh, 0)

    for a in range(3):
        for k in range(9):
            block = wacc[k * O : (k + 1) * O, a * I : (a + 1) * I]
            wsum[:, 9 * a + k] = block.reshape(X, ROWS, I)

    near = core * H
    first = push(
        wsum.at[:, pl.ds((1 - core) * H, H)], w1b, (w1_s, w1_r), 0, (mate, f)
    )

    def backward(d, carry):
        value = product(
            wth[:, : TAPS * O], wtl[:, : TAPS * O],
            sh[pl.ds(d, 3)].reshape(TAPS * O, PLANE), sl[pl.ds(d, 3)].reshape(TAPS * O, PLANE),
            ((1,), (0,)),
        )
        igp[d] = value.reshape(GY, GZ * ROWS, PLANE)
        return carry

    in_sems = (in_s, in_r)
    inward = []

    def input_start(n):
        d, w, way = INPUT_CHUNKS[n]
        planes = pl.ds(d, w)
        lax.fori_loop(d, d + w, backward, 0)
        inward.append(
            {
                "far": push(
                    igp.at[planes, :, rows(z_of(2)), :], zrel.at[planes],
                    in_sems, (n, 0), at_z(way),
                ),
                "back": push(
                    igp.at[planes, :, rows(z_of(-way)), :], zrec.at[1, planes],
                    in_sems, (n, 1), at_z(-way),
                ),
            }
        )

    def input_relay(n):
        d, w, way = INPUT_CHUNKS[n]
        planes = pl.ds(d, w)
        inward[n]["far"].wait_recv()
        igp[planes, :, rows(z_of(way)), :] += zrel[planes]
        inward[n]["on"] = push(
            igp.at[planes, :, rows(z_of(way)), :], zrec.at[0, planes],
            in_sems, (n, 2), at_z(way),
        )

    def input_pair(n):
        d, w, way = INPUT_CHUNKS[n]
        planes = pl.ds(d, w)
        inward[n]["back"].wait_recv()
        inward[n]["on"].wait_recv()
        igp[planes, :, rows(gz), :] += zrec[0, planes] + zrec[1, planes]
        inward[n]["y"] = push(
            igp.at[planes, 1 - gy, rows(gz), :], yrec.at[planes], in_sems, (n, 3), at_y
        )

    def input_end(n):
        d, w, way = INPUT_CHUNKS[n]
        inward[n]["y"].wait_recv()
        for e in range(d, d + w):
            igv[:, e, :] = igp[e, gy, rows(gz), :] + yrec[e]

    wy_sems = (wy_s, wy_r)
    wx_sems = (wx_s, wx_r)
    weights = []

    def weight_start(n):
        t, w, way = TAP_CHUNKS[n]
        part_of = pl.ds(near + t, w)
        wsum[:, part_of] += w1b[:, t : t + w]
        weights.append(
            {
                "y": push(
                    wsum.at[:, part_of], wrel.at[:, pl.ds(t, w)], wy_sems, (n, 0),
                    next_y if way == 1 else prev_y,
                )
            }
        )

    def weight_relay(n):
        t, w, way = TAP_CHUNKS[n]
        weights[n]["y"].wait_recv()
        weights[n]["on"] = push(
            wrel.at[:, pl.ds(t, w)], warr.at[:, pl.ds(t, w)], wy_sems, (n, 1),
            next_y if way == 1 else prev_y,
        )

    scale = 1.0 / math.sqrt(PLANES * SLABS * PLANE)

    def weight_sum(n):
        t, w, way = TAP_CHUNKS[n]
        part_of = pl.ds(near + t, w)
        weights[n]["on"].wait_recv()
        wtot[:, t : t + w] = (wsum[:, part_of] + warr[:, t : t + w]) * scale
        for j in (2, 1, 3):
            weights[n]["x", j] = push(
                wtot.at[x_of(j), pl.ds(t, w)], wout.at[part_of, :, lanes(x)],
                wx_sems, (n, j - 1), at_x(j),
            )
        wout[part_of, :, lanes(x)] = wtot[x, t : t + w]

    def weight_swap(n):
        t, w, way = TAP_CHUNKS[n]
        for j in (1, 2, 3):
            weights[n]["x", j].wait_recv()
        here = wout.at[pl.ds(near + t, w)]
        weights[n]["mate"] = push(here, here, (w5_s, w5_r), n, (mate, f))

    input_start(0)
    first.wait_recv()
    for n in (0, 1, 2, 3):
        weight_start(n)
    input_start(1)
    rim_arrive()
    stack(0, 0)
    stack(PLANES + 1, 0)
    weight_relay(0)
    weight_relay(1)
    input_relay(0)
    input_start(2)
    weight_relay(2)
    weight_relay(3)
    input_relay(1)
    input_start(3)
    input_relay(2)
    weight_sum(0)
    weight_sum(1)
    input_pair(0)
    input_relay(3)
    input_pair(1)
    weight_sum(2)
    weight_sum(3)
    input_pair(2)
    weight_swap(0)
    weight_swap(1)
    input_end(0)
    input_end(1)
    input_pair(3)
    input_end(2)
    weight_swap(2)
    weight_swap(3)
    input_end(3)
    give_ig = pltpu.make_async_copy(igv, ig, local.at[1])
    give_ig.start()
    for n in range(4):
        weights[n]["mate"].wait_recv()
    give_wg = pltpu.make_async_copy(wout.at[pl.ds(0, TAPS)], wg, local.at[2])
    give_wg.start()

    for copy in sent:
        copy.wait_send()
    edge_leave()
    rim_leave()
    give_act.wait()
    give_ig.wait()
    give_wg.wait()


def scratch():
    I = ROWS * G
    O = ROWS * X
    H = PAD // 2
    columns = -(-TAPS * O // 128) * 128
    vmem = pltpu.VMEM
    dma = pltpu.SemaphoreType.DMA
    return [
        vmem((ROWS, PLANES, PLANE), F32),
        vmem((ROWS, PLANES, PLANE), F32),
        vmem((ROWS, PLANES, PLANE), F32),
        vmem((ROWS, PLANES, PLANE), F32),
        vmem((PLANES + 2, GY, GZ * ROWS, PLANE), F32),
        vmem((PLANES + 2, I, PLANE), BF16),
        vmem((PLANES + 2, I, PLANE), BF16),
        vmem((X, TAPS, ROWS, I), F32),
        vmem((9 * O, 3 * I), BF16),
        vmem((9 * O, 3 * I), BF16),
        vmem((columns, I), F32),
        vmem((I, columns), BF16),
        vmem((I, columns), BF16),
        vmem((9 * O, PLANE), F32),
        vmem((PLANES, O, PLANE), F32),
        vmem((X - 1, PLANES, ROWS, PLANE), F32),
        vmem((PLANES + 2, O, PLANE), F32),
        vmem((PLANES + 2, 9 * O, PLANE), BF16),
        vmem((PLANES + 2, 9 * O, PLANE), BF16),
        vmem((9 * O, 3 * I), F32),
        vmem((X, PAD, ROWS, I), F32),
        vmem((X, H, ROWS, I), F32),
        vmem((X, H, ROWS, I), F32),
        vmem((X, H, ROWS, I), F32),
        vmem((X, H, ROWS, I), F32),
        vmem((PAD, ROWS, X * I), F32),
        vmem((PLANES, GY, GZ * ROWS, PLANE), F32),
        vmem((PLANES, GY, ROWS, PLANE), F32),
        vmem((2, PLANES, GY, ROWS, PLANE), F32),
        vmem((PLANES, ROWS, PLANE), F32),
        dma((3,)),
        dma((4, 6)), dma((4, 6)),
        dma((6,)), dma((6,)),
        dma((2,)), dma((2,)),
        dma((4, 3)), dma((4, 3)),
        dma((4, 3)), dma((4, 3)),
        dma((2,)), dma((2,)),
        dma((4, 4)), dma((4, 4)),
        dma((1,)), dma((1,)),
        dma((4, 2)), dma((4, 2)),
        dma((4, 3)), dma((4, 3)),
        dma((4,)), dma((4,)),
    ]


def hand_out(act, ig, wg, act_out, ig_out, wg_out, sems):
    copies = [
        pltpu.make_async_copy(source, target, sems.at[n])
        for n, (source, target) in enumerate(((act, act_out), (ig, ig_out), (wg, wg_out)))
    ]
    for copy in copies:
        copy.start()
    for copy in copies:
        copy.wait()


def shards(volume, filters, out_grad):
    anywhere = pl.BlockSpec(memory_space=pl.ANY)
    shapes = (
        jax.ShapeDtypeStruct(volume.shape, F32),
        jax.ShapeDtypeStruct(volume.shape, F32),
        jax.ShapeDtypeStruct(filters.shape, F32),
    )
    held = pl.pallas_call(
        kernel,
        out_shape=shapes,
        in_specs=[anywhere] * 3,
        out_specs=(anywhere,) * 3,
        scratch_shapes=scratch(),
        compiler_params=pltpu.CompilerParams(
            collective_id=0, has_side_effects=True, vmem_limit_bytes=56 * 2**20
        ),
    )(volume, filters, out_grad)
    return pl.pallas_call(
        hand_out,
        out_shape=shapes,
        in_specs=[pl.BlockSpec(memory_space=pltpu.VMEM)] * 3,
        out_specs=(anywhere,) * 3,
        scratch_shapes=[pltpu.SemaphoreType.DMA((3,))],
    )(*held)


def solution(mesh):
    placed = (P("filt", "slab", None), P(None, "filt", None), P("filt", "slab", None))
    return jax.shard_map(
        shards,
        mesh=mesh,
        in_specs=placed,
        out_specs=(P("filt", "slab", None), P("filt", "slab", None), P(None, "filt", None)),
        check_vma=False,
    )
```

```python
import math

import jax
import jax.numpy as jnp
from jax import lax
from jax.experimental import pallas as pl
from jax.experimental.pallas import tpu as pltpu
from jax.sharding import PartitionSpec as P

TAPS = 27
PAD = 28
WIDTH = 16
PLANE = 256
ROWS = 16
PLANES = 8
SLABS = 4
X, GY, GZ = 4, 2, 4
G = GY * GZ

GATHER_CHUNKS = ((0, 2, 1), (6, 2, -1), (2, 2, 1), (4, 2, -1))
REDUCE_CHUNKS = ((2, 2), (4, 2), (0, 2), (6, 2))
INPUT_CHUNKS = ((2, 2, 1), (4, 2, -1), (0, 2, 1), (6, 2, -1))
TAP_CHUNKS = ((0, 4), (4, 4), (8, 3), (11, 3))

F32 = jnp.float32
BF16 = jnp.bfloat16


def split(value):
    high = value.astype(BF16)
    low = (value - high.astype(F32)).astype(BF16)
    return high, low


def product(left_high, left_low, right_high, right_low, dims):
    left = jnp.concatenate([left_high, left_high, left_low], axis=dims[0][0])
    right = jnp.concatenate([right_high, right_low, right_high], axis=dims[1][0])
    return lax.dot_general(left, right, (dims, ((), ())), preferred_element_type=F32)


def kernel(
    vol, fil, og, act, ig, wg,
    volv, ogv, actv, igv,
    g32, gh, gl, fa, w9h, w9l, wc, wth, wtl, taps, part, prec, pgx, sh, sl,
    wacc, wsum, w1b, warr, wtot, wout, igp, zrel, zrec, yrec,
    local, g_s, g_r, fil_s, fil_r, hal_s, hal_r, rs_s, rs_r, ag_s, ag_r, ph_s, ph_r,
    in_s, in_r, w1_s, w1_r, wy_s, wy_r, wx_s, wx_r, w5_s, w5_r,
):
    I = ROWS * G
    O = ROWS * X
    H = PAD // 2
    s = lax.axis_index("slab")
    f = lax.axis_index("filt")
    x = f // G
    g = f % G
    gy = g // GZ
    gz = g % GZ
    core = s % 2
    half = s // 2
    mate = half * 2 + (1 - core)
    across = (s + 2) % SLABS
    other = (mate + 2) % SLABS

    def x_of(j):
        return (x + j + X) % X

    def z_of(j):
        return (gz + j + GZ) % GZ

    def at_x(j):
        return (s, x_of(j) * G + g)

    def at_z(j):
        return (s, x * G + gy * GZ + z_of(j))

    flipped = x * G + (1 - gy) * GZ + gz
    at_y = (s, flipped)

    def rows(index):
        return pl.ds(pl.multiple_of(index * ROWS, ROWS), ROWS)

    def lanes(index):
        return pl.ds(pl.multiple_of(index * I, I), I)

    barrier = pltpu.get_barrier_semaphore()
    partners = [
        (mate, f), at_y, at_z(1), at_z(-1), at_x(1), at_x(-1), at_x(2), (other, f),
        (across, f),
    ]
    for partner in partners:
        pl.semaphore_signal(
            barrier, inc=1, device_id=partner, device_id_type=pl.DeviceIdType.MESH
        )

    bring_vol = pltpu.make_async_copy(vol, volv, local.at[0])
    bring_og = pltpu.make_async_copy(og, ogv, local.at[1])
    bring_fil = pltpu.make_async_copy(fil.at[:, :, lanes(x)], fa.at[x], local.at[2])
    bring_vol.start()
    bring_og.start()
    bring_fil.start()

    @pl.when(s == 0)
    def _():
        g32[0] = jnp.zeros((GY, GZ * ROWS, PLANE), F32)
        pgx[0] = jnp.zeros((O, PLANE), F32)

    @pl.when(s == SLABS - 1)
    def _():
        g32[PLANES + 1] = jnp.zeros((GY, GZ * ROWS, PLANE), F32)
        pgx[PLANES + 1] = jnp.zeros((O, PLANE), F32)

    wsum[:, TAPS] = jnp.zeros((X, ROWS, I), F32)
    wc[TAPS * O :] = jnp.zeros((wc.shape[0] - TAPS * O, I), F32)
    wacc[...] = jnp.zeros_like(wacc)

    bring_vol.wait()
    for d in range(PLANES):
        g32[1 + d, gy, rows(gz), :] = volv[:, d, :]

    pl.semaphore_wait(barrier, len(partners))

    sent = []
    leaves = []

    def remote(src, dst, send, recv, device):
        return pltpu.make_async_remote_copy(
            src_ref=src, dst_ref=dst, send_sem=send, recv_sem=recv,
            device_id=device, device_id_type=pl.DeviceIdType.MESH,
        )

    def push(src, dst, sems, index, device):
        send, recv = sems
        copy = remote(src, dst, send.at[index], recv.at[index], device)
        copy.start()
        sent.append(copy)
        return copy


    strip = pl.ds(pl.multiple_of(core * (ROWS // 2), ROWS // 2), ROWS // 2)
    fil_sems = (fil_s, fil_r)
    filters = []
    for j in (1, 3, 2):
        filters.append(
            (
                x_of(-j),
                push(
                    fil.at[:, strip, lanes(x_of(j))], fa.at[x, :, strip], fil_sems, j - 1, at_x(j)
                ),
            )
        )
    g_sems = (g_s, g_r)
    gather = []
    for n, (d, w, way) in enumerate(GATHER_CHUNKS):
        here = g32.at[pl.ds(1 + d, w), gy, rows(gz), :]
        gather.append(
            {
                "y": push(here, here, g_sems, (n, 0), at_y),
                ("own", 1): push(here, here, g_sems, (n, 1), at_z(1)),
                ("own", -1): push(here, here, g_sems, (n, 2), at_z(-1)),
            }
        )
    for n, (d, w, way) in enumerate(GATHER_CHUNKS):
        gather[n]["y"].wait_recv()
        here = g32.at[pl.ds(1 + d, w), 1 - gy, rows(gz), :]
        gather[n]["pair", 1] = push(here, here, g_sems, (n, 3), at_z(1))
        gather[n]["pair", -1] = push(here, here, g_sems, (n, 4), at_z(-1))
    for n, (d, w, way) in enumerate(GATHER_CHUNKS):
        gather[n]["own", way].wait_recv()
        gather[n]["pair", way].wait_recv()
        here = g32.at[pl.ds(1 + d, w), :, rows(z_of(-way)), :]
        gather[n]["far"] = push(here, here, g_sems, (n, 5), at_z(way))

    swaps = []
    for n, (source, copy) in enumerate(filters):
        copy.wait_recv()
        here = fa.at[source, :, strip]
        swaps.append(push(here, here, fil_sems, 3 + n, (mate, f)))
    bring_fil.wait()
    for copy in swaps:
        copy.wait_recv()

    for a in range(3):
        for k in range(9):
            block = fa[:, 9 * a + k].reshape(O, I)
            high, low = split(block)
            w9h[k * O : (k + 1) * O, a * I : (a + 1) * I] = high
            w9l[k * O : (k + 1) * O, a * I : (a + 1) * I] = low
            wc[((2 - a) * 9 + k) * O : ((2 - a) * 9 + k + 1) * O, :] = block

    def transpose(n, carry):
        start = pl.multiple_of(n * 128, 128)
        high, low = split(wc[pl.ds(start, 128), :].T)
        wth[:, pl.ds(start, 128)] = high
        wtl[:, pl.ds(start, 128)] = low
        return carry

    def neighbours(buffer, send, recv):
        up = remote(
            buffer.at[PLANES], buffer.at[0], send.at[0], recv.at[0], ((s + 1) % SLABS, f)
        )
        down = remote(
            buffer.at[1], buffer.at[PLANES + 1], send.at[1], recv.at[1], ((s + 3) % SLABS, f)
        )

        def start():
            @pl.when(s < SLABS - 1)
            def _():
                up.start()

            @pl.when(s > 0)
            def _():
                down.start()

        def arrive():
            @pl.when(s > 0)
            def _():
                up.wait_recv()

            @pl.when(s < SLABS - 1)
            def _():
                down.wait_recv()

        def leave():
            @pl.when(s < SLABS - 1)
            def _():
                up.wait_send()

            @pl.when(s > 0)
            def _():
                down.wait_send()

        return start, arrive, leave

    edge_start, edge_arrive, edge_leave = neighbours(g32, hal_s, hal_r)

    def halve(e, carry):
        high, low = split(g32[e].reshape(I, PLANE))
        gh[e] = high
        gl[e] = low
        return carry

    for n, (d, w, way) in enumerate(GATHER_CHUNKS):
        gather[n]["own", -way].wait_recv()
        gather[n]["pair", -way].wait_recv()
        gather[n]["far"].wait_recv()
        if n == 1:
            edge_start()
            leaves.append(edge_leave)
    lax.fori_loop(1, PLANES + 1, halve, 0)

    lane = lax.broadcasted_iota(jnp.int32, (O, PLANE), 1)
    column = lane % WIDTH
    not_left = column >= 1
    not_right = column <= WIDTH - 2
    not_top = lane >= WIDTH
    not_bottom = lane < PLANE - WIDTH

    def forward(d, carry):
        right_high = gh[pl.ds(d, 3)].reshape(3 * I, PLANE)
        right_low = gl[pl.ds(d, 3)].reshape(3 * I, PLANE)
        taps[...] = product(w9h[...], w9l[...], right_high, right_low, ((1,), (0,)))

        def line(b):
            def tap(c):
                k = 3 * b + c
                return taps[k * O : (k + 1) * O, :]

            total = tap(1)
            total += jnp.where(not_left, pltpu.roll(tap(0), 1, 1), 0.0)
            total += jnp.where(not_right, pltpu.roll(tap(2), PLANE - 1, 1), 0.0)
            return total

        total = line(1)
        total += jnp.where(not_top, pltpu.roll(line(0), WIDTH, 1), 0.0)
        total += jnp.where(not_bottom, pltpu.roll(line(2), PLANE - WIDTH, 1), 0.0)
        part[d] = total
        return carry

    rs_sems = (rs_s, rs_r)
    reduce = []

    def reduce_start(n):
        d, w = REDUCE_CHUNKS[n]
        planes = pl.ds(d, w)
        reduce.append(
            [
                push(
                    part.at[planes, rows(x_of(j)), :], prec.at[j - 1, planes],
                    rs_sems, (n, j - 1), at_x(j),
                )
                for j in (2, 1, 3)
            ]
        )

    ag_sems = (ag_s, ag_r)
    spread = []

    def activate(n):
        d, w = REDUCE_CHUNKS[n]
        for copy in reduce[n]:
            copy.wait_recv()
        for e in range(d, d + w):
            total = part[e, rows(x), :] + prec[0, e] + (prec[1, e] + prec[2, e])
            positive = jnp.maximum(total, 0.0)
            actv[:, e, :] = positive * positive
            pgx[1 + e, rows(x), :] = 2.0 * positive * ogv[:, e, :]
        here = pgx.at[pl.ds(1 + d, w), rows(x), :]
        spread.append([push(here, here, ag_sems, (n, j - 1), at_x(j)) for j in (2, 1, 3)])

    for n, (d, w) in enumerate(REDUCE_CHUNKS):
        if n == 2:
            edge_arrive()
            halve(0, 0)
            halve(PLANES + 1, 0)
        lax.fori_loop(d, d + w, forward, 0)
        reduce_start(n)
        if n == 1:
            bring_og.wait()
        if n > 1:
            activate(n - 2)
    lax.fori_loop(0, wc.shape[0] // 128, transpose, 0)
    activate(2)
    activate(3)
    give_act = pltpu.make_async_copy(actv, act, local.at[0])
    give_act.start()

    def stack(e, carry):
        field = pgx[e]
        for b in range(3):
            if b == 0:
                moved = jnp.where(not_bottom, pltpu.roll(field, PLANE - WIDTH, 1), 0.0)
            elif b == 1:
                moved = field
            else:
                moved = jnp.where(not_top, pltpu.roll(field, WIDTH, 1), 0.0)
            for c in range(3):
                if c == 0:
                    last = jnp.where(not_right, pltpu.roll(moved, PLANE - 1, 1), 0.0)
                elif c == 1:
                    last = moved
                else:
                    last = jnp.where(not_left, pltpu.roll(moved, 1, 1), 0.0)
                k = 3 * b + c
                high, low = split(last)
                sh[e, k * O : (k + 1) * O, :] = high
                sl[e, k * O : (k + 1) * O, :] = low
        return carry

    def weigh(d, carry):
        stack(d + 1, 0)
        term = product(
            sh[d + 1], sl[d + 1],
            gh[pl.ds(d, 3)].reshape(3 * I, PLANE), gl[pl.ds(d, 3)].reshape(3 * I, PLANE),
            ((1,), (1,)),
        )
        wacc[...] += term
        return carry

    rim_start, rim_arrive, rim_leave = neighbours(pgx, ph_s, ph_r)
    for n, (d, w) in enumerate(REDUCE_CHUNKS):
        for copy in spread[n]:
            copy.wait_recv()
        if n == 3:
            rim_start()
            leaves.append(rim_leave)
        lax.fori_loop(d, d + w, weigh, 0)

    for a in range(3):
        for k in range(9):
            block = wacc[k * O : (k + 1) * O, a * I : (a + 1) * I]
            wsum[:, 9 * a + k] = block.reshape(X, ROWS, I)

    near = core * H
    first = push(
        wsum.at[:, pl.ds((1 - core) * H, H)], w1b, (w1_s, w1_r), 0, (mate, f)
    )

    def backward(d, carry):
        value = product(
            wth[:, : TAPS * O], wtl[:, : TAPS * O],
            sh[pl.ds(d, 3)].reshape(TAPS * O, PLANE), sl[pl.ds(d, 3)].reshape(TAPS * O, PLANE),
            ((1,), (0,)),
        )
        igp[d] = value.reshape(GY, GZ * ROWS, PLANE)
        return carry

    in_sems = (in_s, in_r)
    inward = []

    def input_start(n):
        d, w, way = INPUT_CHUNKS[n]
        planes = pl.ds(d, w)
        lax.fori_loop(d, d + w, backward, 0)
        inward.append(
            {
                "far": push(
                    igp.at[planes, :, rows(z_of(2)), :], zrel.at[planes],
                    in_sems, (n, 0), at_z(way),
                ),
                "back": push(
                    igp.at[planes, :, rows(z_of(-way)), :], zrec.at[1, planes],
                    in_sems, (n, 1), at_z(-way),
                ),
            }
        )

    def input_relay(n):
        d, w, way = INPUT_CHUNKS[n]
        planes = pl.ds(d, w)
        inward[n]["far"].wait_recv()
        igp[planes, :, rows(z_of(way)), :] += zrel[planes]
        inward[n]["on"] = push(
            igp.at[planes, :, rows(z_of(way)), :], zrec.at[0, planes],
            in_sems, (n, 2), at_z(way),
        )

    def input_pair(n):
        d, w, way = INPUT_CHUNKS[n]
        planes = pl.ds(d, w)
        inward[n]["back"].wait_recv()
        inward[n]["on"].wait_recv()
        igp[planes, :, rows(gz), :] += zrec[0, planes] + zrec[1, planes]
        inward[n]["y"] = push(
            igp.at[planes, 1 - gy, rows(gz), :], yrec.at[planes], in_sems, (n, 3), at_y
        )

    def input_end(n):
        d, w, way = INPUT_CHUNKS[n]
        inward[n]["y"].wait_recv()
        for e in range(d, d + w):
            igv[:, e, :] = igp[e, gy, rows(gz), :] + yrec[e]

    wy_sems = (wy_s, wy_r)
    wx_sems = (wx_s, wx_r)
    weights = []

    def weight_start(n):
        t, w = TAP_CHUNKS[n]
        part_of = pl.ds(near + t, w)
        wsum[:, part_of] += w1b[:, t : t + w]
        weights.append(
            {
                "y": push(
                    wsum.at[:, part_of], warr.at[:, pl.ds(t, w)], wy_sems, n, (across, f)
                )
            }
        )

    scale = 1.0 / math.sqrt(PLANES * SLABS * PLANE)

    def weight_sum(n):
        t, w = TAP_CHUNKS[n]
        part_of = pl.ds(near + t, w)
        weights[n]["y"].wait_recv()
        wtot[:, t : t + w] = (wsum[:, part_of] + warr[:, t : t + w]) * scale
        for j in (2, 1, 3):
            weights[n]["x", j] = push(
                wtot.at[x_of(j), pl.ds(t, w)], wout.at[part_of, :, lanes(x)],
                wx_sems, (n, j - 1), at_x(j),
            )
        wout[part_of, :, lanes(x)] = wtot[x, t : t + w]

    def weight_swap(n):
        t, w = TAP_CHUNKS[n]
        for j in (1, 2, 3):
            weights[n]["x", j].wait_recv()
        here = wout.at[pl.ds(near + t, w)]
        weights[n]["mate"] = push(here, here, (w5_s, w5_r), n, (mate, f))

    input_start(0)
    first.wait_recv()
    for n in (0, 1, 2, 3):
        weight_start(n)
    input_start(1)
    rim_arrive()
    stack(0, 0)
    stack(PLANES + 1, 0)
    input_relay(0)
    input_start(2)
    input_relay(1)
    input_start(3)
    input_relay(2)
    weight_sum(0)
    weight_sum(1)
    input_pair(0)
    input_relay(3)
    input_pair(1)
    weight_sum(2)
    weight_sum(3)
    input_pair(2)
    weight_swap(0)
    weight_swap(1)
    input_end(0)
    input_end(1)
    input_pair(3)
    input_end(2)
    weight_swap(2)
    weight_swap(3)
    input_end(3)
    give_ig = pltpu.make_async_copy(igv, ig, local.at[1])
    give_ig.start()
    for n in range(4):
        weights[n]["mate"].wait_recv()
    give_wg = pltpu.make_async_copy(wout.at[pl.ds(0, TAPS)], wg, local.at[2])
    give_wg.start()

    for copy in sent:
        copy.wait_send()
    edge_leave()
    rim_leave()
    give_act.wait()
    give_ig.wait()
    give_wg.wait()


def scratch():
    I = ROWS * G
    O = ROWS * X
    H = PAD // 2
    columns = -(-TAPS * O // 128) * 128
    vmem = pltpu.VMEM
    dma = pltpu.SemaphoreType.DMA
    return [
        vmem((ROWS, PLANES, PLANE), F32),
        vmem((ROWS, PLANES, PLANE), F32),
        vmem((ROWS, PLANES, PLANE), F32),
        vmem((ROWS, PLANES, PLANE), F32),
        vmem((PLANES + 2, GY, GZ * ROWS, PLANE), F32),
        vmem((PLANES + 2, I, PLANE), BF16),
        vmem((PLANES + 2, I, PLANE), BF16),
        vmem((X, TAPS, ROWS, I), F32),
        vmem((9 * O, 3 * I), BF16),
        vmem((9 * O, 3 * I), BF16),
        vmem((columns, I), F32),
        vmem((I, columns), BF16),
        vmem((I, columns), BF16),
        vmem((9 * O, PLANE), F32),
        vmem((PLANES, O, PLANE), F32),
        vmem((X - 1, PLANES, ROWS, PLANE), F32),
        vmem((PLANES + 2, O, PLANE), F32),
        vmem((PLANES + 2, 9 * O, PLANE), BF16),
        vmem((PLANES + 2, 9 * O, PLANE), BF16),
        vmem((9 * O, 3 * I), F32),
        vmem((X, PAD, ROWS, I), F32),
        vmem((X, H, ROWS, I), F32),
        vmem((X, H, ROWS, I), F32),
        vmem((X, H, ROWS, I), F32),
        vmem((PAD, ROWS, X * I), F32),
        vmem((PLANES, GY, GZ * ROWS, PLANE), F32),
        vmem((PLANES, GY, ROWS, PLANE), F32),
        vmem((2, PLANES, GY, ROWS, PLANE), F32),
        vmem((PLANES, ROWS, PLANE), F32),
        dma((3,)),
        dma((len(GATHER_CHUNKS), 6)), dma((len(GATHER_CHUNKS), 6)),
        dma((6,)), dma((6,)),
        dma((2,)), dma((2,)),
        dma((4, 3)), dma((4, 3)),
        dma((4, 3)), dma((4, 3)),
        dma((2,)), dma((2,)),
        dma((4, 4)), dma((4, 4)),
        dma((1,)), dma((1,)),
        dma((4,)), dma((4,)),
        dma((4, 3)), dma((4, 3)),
        dma((4,)), dma((4,)),
    ]


def hand_out(act, ig, wg, act_out, ig_out, wg_out, sems):
    copies = [
        pltpu.make_async_copy(source, target, sems.at[n])
        for n, (source, target) in enumerate(((act, act_out), (ig, ig_out), (wg, wg_out)))
    ]
    for copy in copies:
        copy.start()
    for copy in copies:
        copy.wait()


def shards(volume, filters, out_grad):
    anywhere = pl.BlockSpec(memory_space=pl.ANY)
    shapes = (
        jax.ShapeDtypeStruct(volume.shape, F32),
        jax.ShapeDtypeStruct(volume.shape, F32),
        jax.ShapeDtypeStruct(filters.shape, F32),
    )
    held = pl.pallas_call(
        kernel,
        out_shape=shapes,
        in_specs=[anywhere] * 3,
        out_specs=(anywhere,) * 3,
        scratch_shapes=scratch(),
        compiler_params=pltpu.CompilerParams(
            collective_id=0, has_side_effects=True, vmem_limit_bytes=56 * 2**20
        ),
    )(volume, filters, out_grad)
    return pl.pallas_call(
        hand_out,
        out_shape=shapes,
        in_specs=[pl.BlockSpec(memory_space=pltpu.VMEM)] * 3,
        out_specs=(anywhere,) * 3,
        scratch_shapes=[pltpu.SemaphoreType.DMA((3,))],
    )(*held)


def solution(mesh):
    placed = (P("filt", "slab", None), P(None, "filt", None), P("filt", "slab", None))
    return jax.shard_map(
        shards,
        mesh=mesh,
        in_specs=placed,
        out_specs=(P("filt", "slab", None), P("filt", "slab", None), P(None, "filt", None)),
        check_vma=False,
    )
```

```python
import math

import jax
import jax.numpy as jnp
from jax import lax
from jax.experimental import pallas as pl
from jax.experimental.pallas import tpu as pltpu
from jax.sharding import PartitionSpec as P

TAPS = 27
PAD = 28
WIDTH = 16
PLANE = 256
ROWS = 16
PLANES = 8
SLABS = 4
X, GY, GZ = 4, 2, 4
G = GY * GZ

GATHER_CHUNKS = ((0, 2, 1), (6, 2, -1), (2, 2, 1), (4, 2, -1))
REDUCE_CHUNKS = ((2, 2), (4, 2), (0, 2), (6, 2))
INPUT_CHUNKS = ((2, 2, 1), (4, 2, -1), (0, 2, 1), (6, 2, -1))
TAP_CHUNKS = ((0, 4), (4, 4), (8, 3), (11, 3))

F32 = jnp.float32
BF16 = jnp.bfloat16


def split(value):
    high = value.astype(BF16)
    low = (value - high.astype(F32)).astype(BF16)
    return high, low


def product(left_high, left_low, right_high, right_low, dims):
    left = jnp.concatenate([left_high, left_high, left_low], axis=dims[0][0])
    right = jnp.concatenate([right_high, right_low, right_high], axis=dims[1][0])
    return lax.dot_general(left, right, (dims, ((), ())), preferred_element_type=F32)


def kernel(
    vol, fil, og, act, ig, wg,
    volv, ogv, actv, igv,
    g32, gh, gl, fa, w9h, w9l, wc, wth, wtl, taps, part, prec, pgx, sh, sl,
    wacc, wsum, w1b, warr, wtot, wout, igp, zrel, zrec, yrec,
    local, g_s, g_r, fil_s, fil_r, hal_s, hal_r, rs_s, rs_r, ag_s, ag_r, ph_s, ph_r,
    in_s, in_r, w1_s, w1_r, wy_s, wy_r, wx_s, wx_r, w5_s, w5_r,
):
    I = ROWS * G
    O = ROWS * X
    H = PAD // 2
    s = lax.axis_index("slab")
    f = lax.axis_index("filt")
    x = f // G
    g = f % G
    gy = g // GZ
    gz = g % GZ
    core = s % 2
    half = s // 2
    mate = half * 2 + (1 - core)
    across = (s + 2) % SLABS
    other = (mate + 2) % SLABS

    def x_of(j):
        return (x + j + X) % X

    def z_of(j):
        return (gz + j + GZ) % GZ

    def at_x(j):
        return (s, x_of(j) * G + g)

    def at_z(j):
        return (s, x * G + gy * GZ + z_of(j))

    flipped = x * G + (1 - gy) * GZ + gz
    at_y = (s, flipped)

    def rows(index):
        return pl.ds(pl.multiple_of(index * ROWS, ROWS), ROWS)

    def lanes(index):
        return pl.ds(pl.multiple_of(index * I, I), I)

    barrier = pltpu.get_barrier_semaphore()
    partners = [
        (mate, f), at_y, at_z(1), at_z(-1), at_x(1), at_x(-1), at_x(2), (other, f),
        (across, f),
    ]
    for partner in partners:
        pl.semaphore_signal(
            barrier, inc=1, device_id=partner, device_id_type=pl.DeviceIdType.MESH
        )

    bring_vol = pltpu.make_async_copy(vol, volv, local.at[0])
    bring_og = pltpu.make_async_copy(og, ogv, local.at[1])
    bring_fil = pltpu.make_async_copy(fil.at[:, :, lanes(x)], fa.at[x], local.at[2])
    bring_vol.start()
    bring_og.start()
    bring_fil.start()

    @pl.when(s == 0)
    def _():
        g32[0] = jnp.zeros((GY, GZ * ROWS, PLANE), F32)
        pgx[0] = jnp.zeros((O, PLANE), F32)

    @pl.when(s == SLABS - 1)
    def _():
        g32[PLANES + 1] = jnp.zeros((GY, GZ * ROWS, PLANE), F32)
        pgx[PLANES + 1] = jnp.zeros((O, PLANE), F32)

    wsum[:, TAPS] = jnp.zeros((X, ROWS, I), F32)
    wc[TAPS * O :] = jnp.zeros((wc.shape[0] - TAPS * O, I), F32)
    wacc[...] = jnp.zeros_like(wacc)

    bring_vol.wait()
    for d in range(PLANES):
        g32[1 + d, gy, rows(gz), :] = volv[:, d, :]

    pl.semaphore_wait(barrier, len(partners))

    sent = []
    leaves = []

    def remote(src, dst, send, recv, device):
        return pltpu.make_async_remote_copy(
            src_ref=src, dst_ref=dst, send_sem=send, recv_sem=recv,
            device_id=device, device_id_type=pl.DeviceIdType.MESH,
        )

    def push(src, dst, sems, index, device):
        send, recv = sems
        copy = remote(src, dst, send.at[index], recv.at[index], device)
        copy.start()
        sent.append(copy)
        return copy


    strip = pl.ds(pl.multiple_of(core * (ROWS // 2), ROWS // 2), ROWS // 2)
    fil_sems = (fil_s, fil_r)
    filters = []
    for j in (1, 3, 2):
        filters.append(
            (
                x_of(-j),
                push(
                    fil.at[:, strip, lanes(x_of(j))], fa.at[x, :, strip], fil_sems, j - 1, at_x(j)
                ),
            )
        )
    g_sems = (g_s, g_r)
    gather = []
    for n, (d, w, way) in enumerate(GATHER_CHUNKS):
        here = g32.at[pl.ds(1 + d, w), gy, rows(gz), :]
        gather.append(
            {
                "y": push(here, here, g_sems, (n, 0), at_y),
                ("own", 1): push(here, here, g_sems, (n, 1), at_z(1)),
                ("own", -1): push(here, here, g_sems, (n, 2), at_z(-1)),
            }
        )
    for n, (d, w, way) in enumerate(GATHER_CHUNKS):
        gather[n]["y"].wait_recv()
        here = g32.at[pl.ds(1 + d, w), 1 - gy, rows(gz), :]
        gather[n]["pair", 1] = push(here, here, g_sems, (n, 3), at_z(1))
        gather[n]["pair", -1] = push(here, here, g_sems, (n, 4), at_z(-1))
    for n, (d, w, way) in enumerate(GATHER_CHUNKS):
        gather[n]["own", way].wait_recv()
        gather[n]["pair", way].wait_recv()
        here = g32.at[pl.ds(1 + d, w), :, rows(z_of(-way)), :]
        gather[n]["far"] = push(here, here, g_sems, (n, 5), at_z(way))

    swaps = []
    for n, (source, copy) in enumerate(filters):
        copy.wait_recv()
        here = fa.at[source, :, strip]
        swaps.append(push(here, here, fil_sems, 3 + n, (mate, f)))
    bring_fil.wait()
    for copy in swaps:
        copy.wait_recv()

    for a in range(3):
        for k in range(9):
            block = fa[:, 9 * a + k].reshape(O, I)
            high, low = split(block)
            w9h[k * O : (k + 1) * O, a * I : (a + 1) * I] = high
            w9l[k * O : (k + 1) * O, a * I : (a + 1) * I] = low
            wc[((2 - a) * 9 + k) * O : ((2 - a) * 9 + k + 1) * O, :] = block

    def transpose(n, carry):
        start = pl.multiple_of(n * 128, 128)
        high, low = split(wc[pl.ds(start, 128), :].T)
        wth[:, pl.ds(start, 128)] = high
        wtl[:, pl.ds(start, 128)] = low
        return carry

    def neighbours(buffer, send, recv):
        up = remote(
            buffer.at[PLANES], buffer.at[0], send.at[0], recv.at[0], ((s + 1) % SLABS, f)
        )
        down = remote(
            buffer.at[1], buffer.at[PLANES + 1], send.at[1], recv.at[1], ((s + 3) % SLABS, f)
        )

        def start():
            @pl.when(s < SLABS - 1)
            def _():
                up.start()

            @pl.when(s > 0)
            def _():
                down.start()

        def arrive():
            @pl.when(s > 0)
            def _():
                up.wait_recv()

            @pl.when(s < SLABS - 1)
            def _():
                down.wait_recv()

        def leave():
            @pl.when(s < SLABS - 1)
            def _():
                up.wait_send()

            @pl.when(s > 0)
            def _():
                down.wait_send()

        return start, arrive, leave

    edge_start, edge_arrive, edge_leave = neighbours(g32, hal_s, hal_r)

    def halve(e, carry):
        high, low = split(g32[e].reshape(I, PLANE))
        gh[e] = high
        gl[e] = low
        return carry

    for n, (d, w, way) in enumerate(GATHER_CHUNKS):
        gather[n]["own", -way].wait_recv()
        gather[n]["pair", -way].wait_recv()
        gather[n]["far"].wait_recv()
        if n == 1:
            edge_start()
            leaves.append(edge_leave)
    lax.fori_loop(1, PLANES + 1, halve, 0)

    lane = lax.broadcasted_iota(jnp.int32, (O, PLANE), 1)
    column = lane % WIDTH
    not_left = column >= 1
    not_right = column <= WIDTH - 2
    not_top = lane >= WIDTH
    not_bottom = lane < PLANE - WIDTH

    def forward(d, carry):
        right_high = gh[pl.ds(d, 3)].reshape(3 * I, PLANE)
        right_low = gl[pl.ds(d, 3)].reshape(3 * I, PLANE)
        taps[...] = product(w9h[...], w9l[...], right_high, right_low, ((1,), (0,)))

        def line(b):
            def tap(c):
                k = 3 * b + c
                return taps[k * O : (k + 1) * O, :]

            total = tap(1)
            total += jnp.where(not_left, pltpu.roll(tap(0), 1, 1), 0.0)
            total += jnp.where(not_right, pltpu.roll(tap(2), PLANE - 1, 1), 0.0)
            return total

        total = line(1)
        total += jnp.where(not_top, pltpu.roll(line(0), WIDTH, 1), 0.0)
        total += jnp.where(not_bottom, pltpu.roll(line(2), PLANE - WIDTH, 1), 0.0)
        part[d] = total
        return carry

    rs_sems = (rs_s, rs_r)
    reduce = []

    def reduce_start(n):
        d, w = REDUCE_CHUNKS[n]
        planes = pl.ds(d, w)
        reduce.append(
            [
                push(
                    part.at[planes, rows(x_of(j)), :], prec.at[j - 1, planes],
                    rs_sems, (n, j - 1), at_x(j),
                )
                for j in (2, 1, 3)
            ]
        )

    ag_sems = (ag_s, ag_r)
    spread = []

    def activate(n):
        d, w = REDUCE_CHUNKS[n]
        for copy in reduce[n]:
            copy.wait_recv()
        for e in range(d, d + w):
            total = part[e, rows(x), :] + prec[0, e] + (prec[1, e] + prec[2, e])
            positive = jnp.maximum(total, 0.0)
            actv[:, e, :] = positive * positive
            pgx[1 + e, rows(x), :] = 2.0 * positive * ogv[:, e, :]
        here = pgx.at[pl.ds(1 + d, w), rows(x), :]
        spread.append([push(here, here, ag_sems, (n, j - 1), at_x(j)) for j in (2, 1, 3)])

    for n, (d, w) in enumerate(REDUCE_CHUNKS):
        if n == 2:
            edge_arrive()
            halve(0, 0)
            halve(PLANES + 1, 0)
        lax.fori_loop(d, d + w, forward, 0)
        reduce_start(n)
        if n == 1:
            bring_og.wait()
        if n > 1:
            activate(n - 2)
    lax.fori_loop(0, wc.shape[0] // 128, transpose, 0)
    activate(2)
    activate(3)
    give_act = pltpu.make_async_copy(actv, act, local.at[0])
    give_act.start()

    def stack(e, carry):
        field = pgx[e]
        for b in range(3):
            if b == 0:
                moved = jnp.where(not_bottom, pltpu.roll(field, PLANE - WIDTH, 1), 0.0)
            elif b == 1:
                moved = field
            else:
                moved = jnp.where(not_top, pltpu.roll(field, WIDTH, 1), 0.0)
            for c in range(3):
                if c == 0:
                    last = jnp.where(not_right, pltpu.roll(moved, PLANE - 1, 1), 0.0)
                elif c == 1:
                    last = moved
                else:
                    last = jnp.where(not_left, pltpu.roll(moved, 1, 1), 0.0)
                k = 3 * b + c
                high, low = split(last)
                sh[e, k * O : (k + 1) * O, :] = high
                sl[e, k * O : (k + 1) * O, :] = low
        return carry

    def weigh(d, carry):
        stack(d + 1, 0)
        term = product(
            sh[d + 1], sl[d + 1],
            gh[pl.ds(d, 3)].reshape(3 * I, PLANE), gl[pl.ds(d, 3)].reshape(3 * I, PLANE),
            ((1,), (1,)),
        )
        wacc[...] += term
        return carry

    rim_start, rim_arrive, rim_leave = neighbours(pgx, ph_s, ph_r)
    for n, (d, w) in enumerate(REDUCE_CHUNKS):
        for copy in spread[n]:
            copy.wait_recv()
        if n == 3:
            rim_start()
            leaves.append(rim_leave)
        lax.fori_loop(d, d + w, weigh, 0)

    for a in range(3):
        for k in range(9):
            block = wacc[k * O : (k + 1) * O, a * I : (a + 1) * I]
            wsum[:, 9 * a + k] = block.reshape(X, ROWS, I)

    near = core * H
    first = push(
        wsum.at[:, pl.ds((1 - core) * H, H)], w1b, (w1_s, w1_r), 0, (mate, f)
    )

    def backward(d, carry):
        value = product(
            wth[:, : TAPS * O], wtl[:, : TAPS * O],
            sh[pl.ds(d, 3)].reshape(TAPS * O, PLANE), sl[pl.ds(d, 3)].reshape(TAPS * O, PLANE),
            ((1,), (0,)),
        )
        igp[d] = value.reshape(GY, GZ * ROWS, PLANE)
        return carry

    in_sems = (in_s, in_r)
    inward = []

    def input_start(n):
        d, w, way = INPUT_CHUNKS[n]
        planes = pl.ds(d, w)
        lax.fori_loop(d, d + w, backward, 0)
        inward.append(
            {
                "far": push(
                    igp.at[planes, :, rows(z_of(2)), :], zrel.at[planes],
                    in_sems, (n, 0), at_z(way),
                ),
                "back": push(
                    igp.at[planes, :, rows(z_of(-way)), :], zrec.at[1, planes],
                    in_sems, (n, 1), at_z(-way),
                ),
            }
        )

    def input_relay(n):
        d, w, way = INPUT_CHUNKS[n]
        planes = pl.ds(d, w)
        inward[n]["far"].wait_recv()
        igp[planes, :, rows(z_of(way)), :] += zrel[planes]
        inward[n]["on"] = push(
            igp.at[planes, :, rows(z_of(way)), :], zrec.at[0, planes],
            in_sems, (n, 2), at_z(way),
        )

    def input_pair(n):
        d, w, way = INPUT_CHUNKS[n]
        planes = pl.ds(d, w)
        inward[n]["back"].wait_recv()
        inward[n]["on"].wait_recv()
        igp[planes, :, rows(gz), :] += zrec[0, planes] + zrec[1, planes]
        inward[n]["y"] = push(
            igp.at[planes, 1 - gy, rows(gz), :], yrec.at[planes], in_sems, (n, 3), at_y
        )

    def input_end(n):
        d, w, way = INPUT_CHUNKS[n]
        inward[n]["y"].wait_recv()
        for e in range(d, d + w):
            igv[:, e, :] = igp[e, gy, rows(gz), :] + yrec[e]

    wy_sems = (wy_s, wy_r)
    wx_sems = (wx_s, wx_r)
    weights = []

    def weight_start(n):
        t, w = TAP_CHUNKS[n]
        part_of = pl.ds(near + t, w)
        wsum[:, part_of] += w1b[:, t : t + w]
        weights.append(
            {
                "y": push(
                    wsum.at[:, part_of], warr.at[:, pl.ds(t, w)], wy_sems, n, (across, f)
                )
            }
        )

    scale = 1.0 / math.sqrt(PLANES * SLABS * PLANE)

    def weight_sum(n):
        t, w = TAP_CHUNKS[n]
        part_of = pl.ds(near + t, w)
        weights[n]["y"].wait_recv()
        wtot[:, t : t + w] = (wsum[:, part_of] + warr[:, t : t + w]) * scale
        for j in (2, 1, 3):
            weights[n]["x", j] = push(
                wtot.at[x_of(j), pl.ds(t, w)], wout.at[part_of, :, lanes(x)],
                wx_sems, (n, j - 1), at_x(j),
            )
        wout[part_of, :, lanes(x)] = wtot[x, t : t + w]

    def weight_swap(n):
        t, w = TAP_CHUNKS[n]
        for j in (1, 2, 3):
            weights[n]["x", j].wait_recv()
        here = wout.at[pl.ds(near + t, w)]
        weights[n]["mate"] = push(here, here, (w5_s, w5_r), n, (mate, f))

    input_start(0)
    first.wait_recv()
    for n in (0, 1, 2, 3):
        weight_start(n)
    input_start(1)
    rim_arrive()
    stack(0, 0)
    stack(PLANES + 1, 0)
    input_relay(0)
    input_start(2)
    input_relay(1)
    input_start(3)
    input_relay(2)
    weight_sum(0)
    weight_sum(1)
    input_pair(0)
    input_relay(3)
    input_pair(1)
    weight_sum(2)
    weight_sum(3)
    input_pair(2)
    weight_swap(0)
    weight_swap(1)
    input_end(0)
    input_end(1)
    input_pair(3)
    input_end(2)
    weight_swap(2)
    weight_swap(3)
    input_end(3)
    give_ig = pltpu.make_async_copy(igv, ig, local.at[1])
    give_ig.start()
    gifts = [give_act, give_ig]
    for n, (t, w) in enumerate(TAP_CHUNKS):
        weights[n]["mate"].wait_recv()
        for k in range(2):
            taps_of = pl.ds(k * H + t, min(w, TAPS - k * H - t))
            give = pltpu.make_async_copy(wout.at[taps_of], wg.at[taps_of], local.at[2 + 2 * n + k])
            give.start()
            gifts.append(give)

    for copy in sent:
        copy.wait_send()
    edge_leave()
    rim_leave()
    for give in gifts:
        give.wait()


def scratch():
    I = ROWS * G
    O = ROWS * X
    H = PAD // 2
    columns = -(-TAPS * O // 128) * 128
    vmem = pltpu.VMEM
    dma = pltpu.SemaphoreType.DMA
    return [
        vmem((ROWS, PLANES, PLANE), F32),
        vmem((ROWS, PLANES, PLANE), F32),
        vmem((ROWS, PLANES, PLANE), F32),
        vmem((ROWS, PLANES, PLANE), F32),
        vmem((PLANES + 2, GY, GZ * ROWS, PLANE), F32),
        vmem((PLANES + 2, I, PLANE), BF16),
        vmem((PLANES + 2, I, PLANE), BF16),
        vmem((X, TAPS, ROWS, I), F32),
        vmem((9 * O, 3 * I), BF16),
        vmem((9 * O, 3 * I), BF16),
        vmem((columns, I), F32),
        vmem((I, columns), BF16),
        vmem((I, columns), BF16),
        vmem((9 * O, PLANE), F32),
        vmem((PLANES, O, PLANE), F32),
        vmem((X - 1, PLANES, ROWS, PLANE), F32),
        vmem((PLANES + 2, O, PLANE), F32),
        vmem((PLANES + 2, 9 * O, PLANE), BF16),
        vmem((PLANES + 2, 9 * O, PLANE), BF16),
        vmem((9 * O, 3 * I), F32),
        vmem((X, PAD, ROWS, I), F32),
        vmem((X, H, ROWS, I), F32),
        vmem((X, H, ROWS, I), F32),
        vmem((X, H, ROWS, I), F32),
        vmem((PAD, ROWS, X * I), F32),
        vmem((PLANES, GY, GZ * ROWS, PLANE), F32),
        vmem((PLANES, GY, ROWS, PLANE), F32),
        vmem((2, PLANES, GY, ROWS, PLANE), F32),
        vmem((PLANES, ROWS, PLANE), F32),
        dma((10,)),
        dma((len(GATHER_CHUNKS), 6)), dma((len(GATHER_CHUNKS), 6)),
        dma((6,)), dma((6,)),
        dma((2,)), dma((2,)),
        dma((4, 3)), dma((4, 3)),
        dma((4, 3)), dma((4, 3)),
        dma((2,)), dma((2,)),
        dma((4, 4)), dma((4, 4)),
        dma((1,)), dma((1,)),
        dma((4,)), dma((4,)),
        dma((4, 3)), dma((4, 3)),
        dma((4,)), dma((4,)),
    ]


def hand_out(act, ig, wg, act_out, ig_out, wg_out, act_held, ig_held, wg_held, into, out):
    parts = [(act, act_held, act_out), (ig, ig_held, ig_out)]
    third = TAPS // 3
    for n in range(3):
        part = pl.ds(n * third, third)
        parts.append((wg.at[part], wg_held.at[part], wg_out.at[part]))
    bring = [pltpu.make_async_copy(p[0], p[1], into.at[n]) for n, p in enumerate(parts)]
    give = [pltpu.make_async_copy(p[1], p[2], out.at[n]) for n, p in enumerate(parts)]
    for copy in bring:
        copy.start()
    for first, second in zip(bring, give):
        first.wait()
        second.start()
    for copy in give:
        copy.wait()


def shards(volume, filters, out_grad):
    anywhere = pl.BlockSpec(memory_space=pl.ANY)
    shapes = (
        jax.ShapeDtypeStruct(volume.shape, F32),
        jax.ShapeDtypeStruct(volume.shape, F32),
        jax.ShapeDtypeStruct(filters.shape, F32),
    )
    held = pl.pallas_call(
        kernel,
        out_shape=shapes,
        in_specs=[anywhere] * 3,
        out_specs=(anywhere,) * 3,
        scratch_shapes=scratch(),
        compiler_params=pltpu.CompilerParams(
            collective_id=0, has_side_effects=True, vmem_limit_bytes=56 * 2**20
        ),
    )(volume, filters, out_grad)
    return pl.pallas_call(
        hand_out,
        out_shape=shapes,
        in_specs=[anywhere] * 3,
        out_specs=(anywhere,) * 3,
        scratch_shapes=[
            *(pltpu.VMEM(shape.shape, F32) for shape in shapes),
            pltpu.SemaphoreType.DMA((5,)), pltpu.SemaphoreType.DMA((5,)),
        ],
    )(*held)


def solution(mesh):
    placed = (P("filt", "slab", None), P(None, "filt", None), P("filt", "slab", None))
    return jax.shard_map(
        shards,
        mesh=mesh,
        in_specs=placed,
        out_specs=(P("filt", "slab", None), P("filt", "slab", None), P(None, "filt", None)),
        check_vma=False,
    )
```

```python
import math

import jax
import jax.numpy as jnp
from jax import lax
from jax.experimental import pallas as pl
from jax.experimental.pallas import tpu as pltpu
from jax.sharding import PartitionSpec as P

TAPS = 27
PAD = 28
WIDTH = 16
PLANE = 256
ROWS = 16
PLANES = 8
SLABS = 4
X, GY, GZ = 4, 2, 4
G = GY * GZ

GATHER_CHUNKS = ((0, 2, 1), (6, 2, -1), (2, 2, 1), (4, 2, -1))
REDUCE_CHUNKS = ((2, 2), (4, 2), (0, 2), (6, 2))
INPUT_CHUNKS = ((2, 2, 1), (4, 2, -1), (0, 2, 1), (6, 2, -1))
TAP_CHUNKS = ((0, 4), (4, 4), (8, 3), (11, 3))

F32 = jnp.float32
BF16 = jnp.bfloat16


def split(value):
    high = value.astype(BF16)
    low = (value - high.astype(F32)).astype(BF16)
    return high, low


def product(left_high, left_low, right_high, right_low, dims):
    left = jnp.concatenate([left_high, left_high, left_low], axis=dims[0][0])
    right = jnp.concatenate([right_high, right_low, right_high], axis=dims[1][0])
    return lax.dot_general(left, right, (dims, ((), ())), preferred_element_type=F32)


def kernel(
    vol, fil, og, act, ig, wg,
    volv, ogv, actv, igv,
    g32, gh, gl, fa, w9h, w9l, wc, wt, taps, part, prec, pgx, sh, sl,
    wacc, wsum, w1b, warr, wtot, wout, igp, zrel, zrec, yrec,
    local, g_s, g_r, fil_s, fil_r, hal_s, hal_r, rs_s, rs_r, ag_s, ag_r, ph_s, ph_r,
    in_s, in_r, w1_s, w1_r, wy_s, wy_r, wx_s, wx_r, w5_s, w5_r,
):
    I = ROWS * G
    O = ROWS * X
    H = PAD // 2
    s = lax.axis_index("slab")
    f = lax.axis_index("filt")
    x = f // G
    g = f % G
    gy = g // GZ
    gz = g % GZ
    core = s % 2
    half = s // 2
    mate = half * 2 + (1 - core)
    across = (s + 2) % SLABS
    other = (mate + 2) % SLABS

    def x_of(j):
        return (x + j + X) % X

    def z_of(j):
        return (gz + j + GZ) % GZ

    def at_x(j):
        return (s, x_of(j) * G + g)

    def at_z(j):
        return (s, x * G + gy * GZ + z_of(j))

    flipped = x * G + (1 - gy) * GZ + gz
    at_y = (s, flipped)

    def rows(index):
        return pl.ds(pl.multiple_of(index * ROWS, ROWS), ROWS)

    def lanes(index):
        return pl.ds(pl.multiple_of(index * I, I), I)

    barrier = pltpu.get_barrier_semaphore()
    partners = [
        (mate, f), at_y, at_z(1), at_z(-1), at_x(1), at_x(-1), at_x(2), (other, f),
        (across, f),
    ]
    for partner in partners:
        pl.semaphore_signal(
            barrier, inc=1, device_id=partner, device_id_type=pl.DeviceIdType.MESH
        )

    bring_vol = pltpu.make_async_copy(vol, volv, local.at[0])
    bring_og = pltpu.make_async_copy(og, ogv, local.at[1])
    bring_fil = pltpu.make_async_copy(fil.at[:, :, lanes(x)], fa.at[x], local.at[2])
    bring_vol.start()
    bring_og.start()
    bring_fil.start()

    @pl.when(s == 0)
    def _():
        g32[0] = jnp.zeros((GY, GZ * ROWS, PLANE), F32)
        pgx[0] = jnp.zeros((O, PLANE), F32)

    @pl.when(s == SLABS - 1)
    def _():
        g32[PLANES + 1] = jnp.zeros((GY, GZ * ROWS, PLANE), F32)
        pgx[PLANES + 1] = jnp.zeros((O, PLANE), F32)

    wsum[:, TAPS] = jnp.zeros((X, ROWS, I), F32)
    wc[TAPS * O :] = jnp.zeros((wc.shape[0] - TAPS * O, I), F32)
    wacc[...] = jnp.zeros_like(wacc)

    bring_vol.wait()
    for d in range(PLANES):
        g32[1 + d, gy, rows(gz), :] = volv[:, d, :]

    pl.semaphore_wait(barrier, len(partners))

    sent = []
    leaves = []

    def remote(src, dst, send, recv, device):
        return pltpu.make_async_remote_copy(
            src_ref=src, dst_ref=dst, send_sem=send, recv_sem=recv,
            device_id=device, device_id_type=pl.DeviceIdType.MESH,
        )

    def push(src, dst, sems, index, device):
        send, recv = sems
        copy = remote(src, dst, send.at[index], recv.at[index], device)
        copy.start()
        sent.append(copy)
        return copy


    strip = pl.ds(pl.multiple_of(core * (ROWS // 2), ROWS // 2), ROWS // 2)
    fil_sems = (fil_s, fil_r)
    filters = []
    for j in (1, 3, 2):
        filters.append(
            (
                x_of(-j),
                push(
                    fil.at[:, strip, lanes(x_of(j))], fa.at[x, :, strip], fil_sems, j - 1, at_x(j)
                ),
            )
        )
    g_sems = (g_s, g_r)
    gather = []
    for n, (d, w, way) in enumerate(GATHER_CHUNKS):
        here = g32.at[pl.ds(1 + d, w), gy, rows(gz), :]
        gather.append(
            {
                "y": push(here, here, g_sems, (n, 0), at_y),
                ("own", 1): push(here, here, g_sems, (n, 1), at_z(1)),
                ("own", -1): push(here, here, g_sems, (n, 2), at_z(-1)),
            }
        )
    for n, (d, w, way) in enumerate(GATHER_CHUNKS):
        gather[n]["y"].wait_recv()
        here = g32.at[pl.ds(1 + d, w), 1 - gy, rows(gz), :]
        gather[n]["pair", 1] = push(here, here, g_sems, (n, 3), at_z(1))
        gather[n]["pair", -1] = push(here, here, g_sems, (n, 4), at_z(-1))
    for n, (d, w, way) in enumerate(GATHER_CHUNKS):
        gather[n]["own", way].wait_recv()
        gather[n]["pair", way].wait_recv()
        here = g32.at[pl.ds(1 + d, w), :, rows(z_of(-way)), :]
        gather[n]["far"] = push(here, here, g_sems, (n, 5), at_z(way))

    swaps = []
    for n, (source, copy) in enumerate(filters):
        copy.wait_recv()
        here = fa.at[source, :, strip]
        swaps.append(push(here, here, fil_sems, 3 + n, (mate, f)))
    bring_fil.wait()
    for copy in swaps:
        copy.wait_recv()

    for a in range(3):
        for k in range(9):
            block = fa[:, 9 * a + k].reshape(O, I)
            high, low = split(block)
            w9h[k * O : (k + 1) * O, a * I : (a + 1) * I] = high
            w9l[k * O : (k + 1) * O, a * I : (a + 1) * I] = low
            wc[((2 - a) * 9 + k) * O : ((2 - a) * 9 + k + 1) * O, :] = block

    def transpose(n, carry):
        start = pl.multiple_of(n * 128, 128)
        high, low = split(wc[pl.ds(start, 128), :].T)
        wt[:I, pl.ds(start, 128)] = high
        wt[I:, pl.ds(start, 128)] = low
        return carry

    def neighbours(buffer, send, recv):
        up = remote(
            buffer.at[PLANES], buffer.at[0], send.at[0], recv.at[0], ((s + 1) % SLABS, f)
        )
        down = remote(
            buffer.at[1], buffer.at[PLANES + 1], send.at[1], recv.at[1], ((s + 3) % SLABS, f)
        )

        def start():
            @pl.when(s < SLABS - 1)
            def _():
                up.start()

            @pl.when(s > 0)
            def _():
                down.start()

        def arrive():
            @pl.when(s > 0)
            def _():
                up.wait_recv()

            @pl.when(s < SLABS - 1)
            def _():
                down.wait_recv()

        def leave():
            @pl.when(s < SLABS - 1)
            def _():
                up.wait_send()

            @pl.when(s > 0)
            def _():
                down.wait_send()

        return start, arrive, leave

    edge_start, edge_arrive, edge_leave = neighbours(g32, hal_s, hal_r)

    def halve(e, carry):
        high, low = split(g32[e].reshape(I, PLANE))
        gh[e] = high
        gl[e] = low
        return carry

    for n, (d, w, way) in enumerate(GATHER_CHUNKS):
        gather[n]["own", -way].wait_recv()
        gather[n]["pair", -way].wait_recv()
        gather[n]["far"].wait_recv()
        if n == 1:
            edge_start()
            leaves.append(edge_leave)
    lax.fori_loop(1, PLANES + 1, halve, 0)

    lane = lax.broadcasted_iota(jnp.int32, (O, PLANE), 1)
    column = lane % WIDTH
    not_left = column >= 1
    not_right = column <= WIDTH - 2
    not_top = lane >= WIDTH
    not_bottom = lane < PLANE - WIDTH

    def forward(d, carry):
        right_high = gh[pl.ds(d, 3)].reshape(3 * I, PLANE)
        right_low = gl[pl.ds(d, 3)].reshape(3 * I, PLANE)
        taps[...] = product(w9h[...], w9l[...], right_high, right_low, ((1,), (0,)))

        def line(b):
            def tap(c):
                k = 3 * b + c
                return taps[k * O : (k + 1) * O, :]

            total = tap(1)
            total += jnp.where(not_left, pltpu.roll(tap(0), 1, 1), 0.0)
            total += jnp.where(not_right, pltpu.roll(tap(2), PLANE - 1, 1), 0.0)
            return total

        total = line(1)
        total += jnp.where(not_top, pltpu.roll(line(0), WIDTH, 1), 0.0)
        total += jnp.where(not_bottom, pltpu.roll(line(2), PLANE - WIDTH, 1), 0.0)
        part[d] = total
        return carry

    rs_sems = (rs_s, rs_r)
    reduce = []

    def reduce_start(n):
        d, w = REDUCE_CHUNKS[n]
        planes = pl.ds(d, w)
        reduce.append(
            [
                push(
                    part.at[planes, rows(x_of(j)), :], prec.at[j - 1, planes],
                    rs_sems, (n, j - 1), at_x(j),
                )
                for j in (2, 1, 3)
            ]
        )

    ag_sems = (ag_s, ag_r)
    spread = []

    def activate(n):
        d, w = REDUCE_CHUNKS[n]
        for copy in reduce[n]:
            copy.wait_recv()
        for e in range(d, d + w):
            total = part[e, rows(x), :] + prec[0, e] + (prec[1, e] + prec[2, e])
            positive = jnp.maximum(total, 0.0)
            actv[:, e, :] = positive * positive
            pgx[1 + e, rows(x), :] = 2.0 * positive * ogv[:, e, :]
        here = pgx.at[pl.ds(1 + d, w), rows(x), :]
        spread.append([push(here, here, ag_sems, (n, j - 1), at_x(j)) for j in (2, 1, 3)])

    for n, (d, w) in enumerate(REDUCE_CHUNKS):
        if n == 2:
            edge_arrive()
            halve(0, 0)
            halve(PLANES + 1, 0)
        lax.fori_loop(d, d + w, forward, 0)
        reduce_start(n)
        if n == 1:
            bring_og.wait()
        if n > 1:
            activate(n - 2)
    lax.fori_loop(0, wc.shape[0] // 128, transpose, 0)
    activate(2)
    activate(3)
    give_act = pltpu.make_async_copy(actv, act, local.at[0])
    give_act.start()

    def stack(e, carry):
        field = pgx[e]
        for b in range(3):
            if b == 0:
                moved = jnp.where(not_bottom, pltpu.roll(field, PLANE - WIDTH, 1), 0.0)
            elif b == 1:
                moved = field
            else:
                moved = jnp.where(not_top, pltpu.roll(field, WIDTH, 1), 0.0)
            for c in range(3):
                if c == 0:
                    last = jnp.where(not_right, pltpu.roll(moved, PLANE - 1, 1), 0.0)
                elif c == 1:
                    last = moved
                else:
                    last = jnp.where(not_left, pltpu.roll(moved, 1, 1), 0.0)
                k = 3 * b + c
                high, low = split(last)
                sh[e, k * O : (k + 1) * O, :] = high
                sl[e, k * O : (k + 1) * O, :] = low
        return carry

    def weigh(d, w):
        lax.fori_loop(d + 1, d + 1 + w, stack, 0)

        def fields(stacked):
            return jnp.concatenate([stacked[e] for e in range(d + 1, d + 1 + w)], axis=1)

        def inputs(held):
            return jnp.concatenate(
                [held[e : e + 3].reshape(3 * I, PLANE) for e in range(d, d + w)], axis=1
            )

        wacc[...] += product(fields(sh), fields(sl), inputs(gh), inputs(gl), ((1,), (1,)))

    rim_start, rim_arrive, rim_leave = neighbours(pgx, ph_s, ph_r)
    for n, (d, w) in enumerate(REDUCE_CHUNKS):
        for copy in spread[n]:
            copy.wait_recv()
        if n == 3:
            rim_start()
            leaves.append(rim_leave)
        weigh(d, w)

    for a in range(3):
        for k in range(9):
            block = wacc[k * O : (k + 1) * O, a * I : (a + 1) * I]
            wsum[:, 9 * a + k] = block.reshape(X, ROWS, I)

    near = core * H
    first = push(
        wsum.at[:, pl.ds((1 - core) * H, H)], w1b, (w1_s, w1_r), 0, (mate, f)
    )

    def backward(d, carry):
        high = jnp.dot(
            wt[:, : TAPS * O], sh[pl.ds(d, 3)].reshape(TAPS * O, PLANE),
            preferred_element_type=F32,
        )
        low = jnp.dot(
            wt[:I, : TAPS * O], sl[pl.ds(d, 3)].reshape(TAPS * O, PLANE),
            preferred_element_type=F32,
        )
        value = high[:I] + (high[I:] + low)
        igp[d] = value.reshape(GY, GZ * ROWS, PLANE)
        return carry

    in_sems = (in_s, in_r)
    inward = []

    def input_start(n):
        d, w, way = INPUT_CHUNKS[n]
        planes = pl.ds(d, w)
        lax.fori_loop(d, d + w, backward, 0)
        inward.append(
            {
                "far": push(
                    igp.at[planes, :, rows(z_of(2)), :], zrel.at[planes],
                    in_sems, (n, 0), at_z(way),
                ),
                "back": push(
                    igp.at[planes, :, rows(z_of(-way)), :], zrec.at[1, planes],
                    in_sems, (n, 1), at_z(-way),
                ),
            }
        )

    def input_relay(n):
        d, w, way = INPUT_CHUNKS[n]
        planes = pl.ds(d, w)
        inward[n]["far"].wait_recv()
        igp[planes, :, rows(z_of(way)), :] += zrel[planes]
        inward[n]["on"] = push(
            igp.at[planes, :, rows(z_of(way)), :], zrec.at[0, planes],
            in_sems, (n, 2), at_z(way),
        )

    def input_pair(n):
        d, w, way = INPUT_CHUNKS[n]
        planes = pl.ds(d, w)
        inward[n]["back"].wait_recv()
        inward[n]["on"].wait_recv()
        igp[planes, :, rows(gz), :] += zrec[0, planes] + zrec[1, planes]
        inward[n]["y"] = push(
            igp.at[planes, 1 - gy, rows(gz), :], yrec.at[planes], in_sems, (n, 3), at_y
        )

    def input_end(n):
        d, w, way = INPUT_CHUNKS[n]
        inward[n]["y"].wait_recv()
        for e in range(d, d + w):
            igv[:, e, :] = igp[e, gy, rows(gz), :] + yrec[e]

    wy_sems = (wy_s, wy_r)
    wx_sems = (wx_s, wx_r)
    weights = []

    def weight_start(n):
        t, w = TAP_CHUNKS[n]
        part_of = pl.ds(near + t, w)
        wsum[:, part_of] += w1b[:, t : t + w]
        weights.append(
            {
                "y": push(
                    wsum.at[:, part_of], warr.at[:, pl.ds(t, w)], wy_sems, n, (across, f)
                )
            }
        )

    scale = 1.0 / math.sqrt(PLANES * SLABS * PLANE)

    def weight_sum(n):
        t, w = TAP_CHUNKS[n]
        part_of = pl.ds(near + t, w)
        weights[n]["y"].wait_recv()
        wtot[:, t : t + w] = (wsum[:, part_of] + warr[:, t : t + w]) * scale
        for j in (2, 1, 3):
            weights[n]["x", j] = push(
                wtot.at[x_of(j), pl.ds(t, w)], wout.at[part_of, :, lanes(x)],
                wx_sems, (n, j - 1), at_x(j),
            )
        wout[part_of, :, lanes(x)] = wtot[x, t : t + w]

    def weight_swap(n):
        t, w = TAP_CHUNKS[n]
        for j in (1, 2, 3):
            weights[n]["x", j].wait_recv()
        here = wout.at[pl.ds(near + t, w)]
        weights[n]["mate"] = push(here, here, (w5_s, w5_r), n, (mate, f))

    input_start(0)
    first.wait_recv()
    for n in (0, 1, 2, 3):
        weight_start(n)
    input_start(1)
    rim_arrive()
    stack(0, 0)
    stack(PLANES + 1, 0)
    input_relay(0)
    input_start(2)
    input_relay(1)
    input_start(3)
    input_relay(2)
    weight_sum(0)
    weight_sum(1)
    input_pair(0)
    input_relay(3)
    input_pair(1)
    weight_sum(2)
    weight_sum(3)
    input_pair(2)
    weight_swap(0)
    weight_swap(1)
    input_end(0)
    input_end(1)
    input_pair(3)
    input_end(2)
    weight_swap(2)
    weight_swap(3)
    input_end(3)
    give_ig = pltpu.make_async_copy(igv, ig, local.at[1])
    give_ig.start()
    gifts = [give_act, give_ig]
    for n, (t, w) in enumerate(TAP_CHUNKS):
        weights[n]["mate"].wait_recv()
        for k in range(2):
            taps_of = pl.ds(k * H + t, min(w, TAPS - k * H - t))
            give = pltpu.make_async_copy(wout.at[taps_of], wg.at[taps_of], local.at[2 + 2 * n + k])
            give.start()
            gifts.append(give)

    for copy in sent:
        copy.wait_send()
    edge_leave()
    rim_leave()
    for give in gifts:
        give.wait()


def scratch():
    I = ROWS * G
    O = ROWS * X
    H = PAD // 2
    columns = -(-TAPS * O // 128) * 128
    vmem = pltpu.VMEM
    dma = pltpu.SemaphoreType.DMA
    return [
        vmem((ROWS, PLANES, PLANE), F32),
        vmem((ROWS, PLANES, PLANE), F32),
        vmem((ROWS, PLANES, PLANE), F32),
        vmem((ROWS, PLANES, PLANE), F32),
        vmem((PLANES + 2, GY, GZ * ROWS, PLANE), F32),
        vmem((PLANES + 2, I, PLANE), BF16),
        vmem((PLANES + 2, I, PLANE), BF16),
        vmem((X, TAPS, ROWS, I), F32),
        vmem((9 * O, 3 * I), BF16),
        vmem((9 * O, 3 * I), BF16),
        vmem((columns, I), F32),
        vmem((2 * I, columns), BF16),
        vmem((9 * O, PLANE), F32),
        vmem((PLANES, O, PLANE), F32),
        vmem((X - 1, PLANES, ROWS, PLANE), F32),
        vmem((PLANES + 2, O, PLANE), F32),
        vmem((PLANES + 2, 9 * O, PLANE), BF16),
        vmem((PLANES + 2, 9 * O, PLANE), BF16),
        vmem((9 * O, 3 * I), F32),
        vmem((X, PAD, ROWS, I), F32),
        vmem((X, H, ROWS, I), F32),
        vmem((X, H, ROWS, I), F32),
        vmem((X, H, ROWS, I), F32),
        vmem((PAD, ROWS, X * I), F32),
        vmem((PLANES, GY, GZ * ROWS, PLANE), F32),
        vmem((PLANES, GY, ROWS, PLANE), F32),
        vmem((2, PLANES, GY, ROWS, PLANE), F32),
        vmem((PLANES, ROWS, PLANE), F32),
        dma((10,)),
        dma((len(GATHER_CHUNKS), 6)), dma((len(GATHER_CHUNKS), 6)),
        dma((6,)), dma((6,)),
        dma((2,)), dma((2,)),
        dma((4, 3)), dma((4, 3)),
        dma((4, 3)), dma((4, 3)),
        dma((2,)), dma((2,)),
        dma((4, 4)), dma((4, 4)),
        dma((1,)), dma((1,)),
        dma((4,)), dma((4,)),
        dma((4, 3)), dma((4, 3)),
        dma((4,)), dma((4,)),
    ]


def hand_out(act, ig, wg, act_out, ig_out, wg_out, act_held, ig_held, wg_held, into, out):
    parts = [(act, act_held, act_out), (ig, ig_held, ig_out)]
    third = TAPS // 3
    for n in range(3):
        part = pl.ds(n * third, third)
        parts.append((wg.at[part], wg_held.at[part], wg_out.at[part]))
    bring = [pltpu.make_async_copy(p[0], p[1], into.at[n]) for n, p in enumerate(parts)]
    give = [pltpu.make_async_copy(p[1], p[2], out.at[n]) for n, p in enumerate(parts)]
    for copy in bring:
        copy.start()
    for first, second in zip(bring, give):
        first.wait()
        second.start()
    for copy in give:
        copy.wait()


def shards(volume, filters, out_grad):
    anywhere = pl.BlockSpec(memory_space=pl.ANY)
    shapes = (
        jax.ShapeDtypeStruct(volume.shape, F32),
        jax.ShapeDtypeStruct(volume.shape, F32),
        jax.ShapeDtypeStruct(filters.shape, F32),
    )
    held = pl.pallas_call(
        kernel,
        out_shape=shapes,
        in_specs=[anywhere] * 3,
        out_specs=(anywhere,) * 3,
        scratch_shapes=scratch(),
        compiler_params=pltpu.CompilerParams(
            collective_id=0, has_side_effects=True, vmem_limit_bytes=56 * 2**20
        ),
    )(volume, filters, out_grad)
    return pl.pallas_call(
        hand_out,
        out_shape=shapes,
        in_specs=[anywhere] * 3,
        out_specs=(anywhere,) * 3,
        scratch_shapes=[
            *(pltpu.VMEM(shape.shape, F32) for shape in shapes),
            pltpu.SemaphoreType.DMA((5,)), pltpu.SemaphoreType.DMA((5,)),
        ],
    )(*held)


def solution(mesh):
    placed = (P("filt", "slab", None), P(None, "filt", None), P("filt", "slab", None))
    return jax.shard_map(
        shards,
        mesh=mesh,
        in_specs=placed,
        out_specs=(P("filt", "slab", None), P("filt", "slab", None), P(None, "filt", None)),
        check_vma=False,
    )
```

```python
import math

import jax
import jax.numpy as jnp
from jax import lax
from jax.experimental import pallas as pl
from jax.experimental.pallas import tpu as pltpu
from jax.sharding import PartitionSpec as P

TAPS = 27
PAD = 28
WIDTH = 16
PLANE = 256
ROWS = 16
PLANES = 8
SLABS = 4
X, GY, GZ = 4, 2, 4
G = GY * GZ

GATHER_CHUNKS = ((0, 2, 1), (6, 2, -1), (2, 2, 1), (4, 2, -1))
REDUCE_CHUNKS = ((2, 2), (4, 2), (0, 2), (6, 2))
INPUT_CHUNKS = ((2, 2, 1), (4, 2, -1), (0, 2, 1), (6, 2, -1))
TAP_CHUNKS = ((0, 4), (4, 4), (8, 3), (11, 3))

F32 = jnp.float32
BF16 = jnp.bfloat16


def split(value):
    high = value.astype(BF16)
    low = (value - high.astype(F32)).astype(BF16)
    return high, low


def product(left_high, left_low, right_high, right_low, dims):
    left = jnp.concatenate([left_high, left_high, left_low], axis=dims[0][0])
    right = jnp.concatenate([right_high, right_low, right_high], axis=dims[1][0])
    return lax.dot_general(left, right, (dims, ((), ())), preferred_element_type=F32)


def kernel(
    vol, fil, og, act, ig, wg,
    volv, ogv, actv, igv,
    g32, gh, gl, fa, w9h, w9l, wc, wt, taps, part, prec, pgx, sh, sl,
    wacc, wsum, w1b, warr, wtot, wout, igp, zrel, zrec, yrec,
    local, g_s, g_r, fil_s, fil_r, hal_s, hal_r, rs_s, rs_r, ag_s, ag_r, ph_s, ph_r,
    in_s, in_r, w1_s, w1_r, wy_s, wy_r, wx_s, wx_r, w5_s, w5_r,
):
    I = ROWS * G
    O = ROWS * X
    H = PAD // 2
    s = lax.axis_index("slab")
    f = lax.axis_index("filt")
    x = f // G
    g = f % G
    gy = g // GZ
    gz = g % GZ
    core = s % 2
    half = s // 2
    mate = half * 2 + (1 - core)
    across = (s + 2) % SLABS
    other = (mate + 2) % SLABS

    def x_of(j):
        return (x + j + X) % X

    def z_of(j):
        return (gz + j + GZ) % GZ

    def at_x(j):
        return (s, x_of(j) * G + g)

    def at_z(j):
        return (s, x * G + gy * GZ + z_of(j))

    flipped = x * G + (1 - gy) * GZ + gz
    at_y = (s, flipped)

    def rows(index):
        return pl.ds(pl.multiple_of(index * ROWS, ROWS), ROWS)

    def lanes(index):
        return pl.ds(pl.multiple_of(index * I, I), I)

    barrier = pltpu.get_barrier_semaphore()
    partners = [
        (mate, f), at_y, at_z(1), at_z(-1), at_x(1), at_x(-1), at_x(2), (other, f),
        (across, f),
    ]
    for partner in partners:
        pl.semaphore_signal(
            barrier, inc=1, device_id=partner, device_id_type=pl.DeviceIdType.MESH
        )

    bring_vol = pltpu.make_async_copy(vol, volv, local.at[0])
    bring_og = pltpu.make_async_copy(og, ogv, local.at[1])
    bring_fil = pltpu.make_async_copy(fil.at[:, :, lanes(x)], fa.at[x], local.at[2])
    bring_vol.start()
    bring_og.start()
    bring_fil.start()

    @pl.when(s == 0)
    def _():
        g32[0] = jnp.zeros((GY, GZ * ROWS, PLANE), F32)
        pgx[0] = jnp.zeros((O, PLANE), F32)

    @pl.when(s == SLABS - 1)
    def _():
        g32[PLANES + 1] = jnp.zeros((GY, GZ * ROWS, PLANE), F32)
        pgx[PLANES + 1] = jnp.zeros((O, PLANE), F32)

    wsum[:, TAPS] = jnp.zeros((X, ROWS, I), F32)
    wc[TAPS * O :] = jnp.zeros((wc.shape[0] - TAPS * O, I), F32)
    wacc[...] = jnp.zeros_like(wacc)

    bring_vol.wait()
    for d in range(PLANES):
        g32[1 + d, gy, rows(gz), :] = volv[:, d, :]

    pl.semaphore_wait(barrier, len(partners))

    sent = []
    leaves = []

    def remote(src, dst, send, recv, device):
        return pltpu.make_async_remote_copy(
            src_ref=src, dst_ref=dst, send_sem=send, recv_sem=recv,
            device_id=device, device_id_type=pl.DeviceIdType.MESH,
        )

    def push(src, dst, sems, index, device):
        send, recv = sems
        copy = remote(src, dst, send.at[index], recv.at[index], device)
        copy.start()
        sent.append(copy)
        return copy


    strip = pl.ds(pl.multiple_of(core * (ROWS // 2), ROWS // 2), ROWS // 2)
    fil_sems = (fil_s, fil_r)
    g_sems = (g_s, g_r)
    gather = []
    for n, (d, w, way) in enumerate(GATHER_CHUNKS):
        here = g32.at[pl.ds(1 + d, w), gy, rows(gz), :]
        gather.append(
            {
                "y": push(here, here, g_sems, (n, 0), at_y),
                ("own", 1): push(here, here, g_sems, (n, 1), at_z(1)),
                ("own", -1): push(here, here, g_sems, (n, 2), at_z(-1)),
            }
        )
    filters = []
    for j in (1, 3, 2):
        filters.append(
            (
                x_of(-j),
                push(
                    fil.at[:, strip, lanes(x_of(j))], fa.at[x, :, strip], fil_sems, j - 1, at_x(j)
                ),
            )
        )
    for n, (d, w, way) in enumerate(GATHER_CHUNKS):
        gather[n]["y"].wait_recv()
        here = g32.at[pl.ds(1 + d, w), 1 - gy, rows(gz), :]
        gather[n]["pair", 1] = push(here, here, g_sems, (n, 3), at_z(1))
        gather[n]["pair", -1] = push(here, here, g_sems, (n, 4), at_z(-1))
    for n, (d, w, way) in enumerate(GATHER_CHUNKS):
        gather[n]["own", way].wait_recv()
        gather[n]["pair", way].wait_recv()
        here = g32.at[pl.ds(1 + d, w), :, rows(z_of(-way)), :]
        gather[n]["far"] = push(here, here, g_sems, (n, 5), at_z(way))

    swaps = []
    for n, (source, copy) in enumerate(filters):
        copy.wait_recv()
        here = fa.at[source, :, strip]
        swaps.append(push(here, here, fil_sems, 3 + n, (mate, f)))
    bring_fil.wait()
    for copy in swaps:
        copy.wait_recv()

    for a in range(3):
        for k in range(9):
            block = fa[:, 9 * a + k].reshape(O, I)
            high, low = split(block)
            w9h[k * O : (k + 1) * O, a * I : (a + 1) * I] = high
            w9l[k * O : (k + 1) * O, a * I : (a + 1) * I] = low
            wc[((2 - a) * 9 + k) * O : ((2 - a) * 9 + k + 1) * O, :] = block

    def transpose(n, carry):
        start = pl.multiple_of(n * 128, 128)
        high, low = split(wc[pl.ds(start, 128), :].T)
        wt[:I, pl.ds(start, 128)] = high
        wt[I:, pl.ds(start, 128)] = low
        return carry

    def neighbours(buffer, send, recv):
        up = remote(
            buffer.at[PLANES], buffer.at[0], send.at[0], recv.at[0], ((s + 1) % SLABS, f)
        )
        down = remote(
            buffer.at[1], buffer.at[PLANES + 1], send.at[1], recv.at[1], ((s + 3) % SLABS, f)
        )

        def start():
            @pl.when(s < SLABS - 1)
            def _():
                up.start()

            @pl.when(s > 0)
            def _():
                down.start()

        def arrive():
            @pl.when(s > 0)
            def _():
                up.wait_recv()

            @pl.when(s < SLABS - 1)
            def _():
                down.wait_recv()

        def leave():
            @pl.when(s < SLABS - 1)
            def _():
                up.wait_send()

            @pl.when(s > 0)
            def _():
                down.wait_send()

        return start, arrive, leave

    edge_start, edge_arrive, edge_leave = neighbours(g32, hal_s, hal_r)

    def halve(e, carry):
        high, low = split(g32[e].reshape(I, PLANE))
        gh[e] = high
        gl[e] = low
        return carry

    for n, (d, w, way) in enumerate(GATHER_CHUNKS):
        gather[n]["own", -way].wait_recv()
        gather[n]["pair", -way].wait_recv()
        gather[n]["far"].wait_recv()
        if n == 1:
            edge_start()
            leaves.append(edge_leave)
    lax.fori_loop(1, PLANES + 1, halve, 0)

    lane = lax.broadcasted_iota(jnp.int32, (O, PLANE), 1)
    column = lane % WIDTH
    not_left = column >= 1
    not_right = column <= WIDTH - 2
    not_top = lane >= WIDTH
    not_bottom = lane < PLANE - WIDTH

    def forward(d, carry):
        right_high = gh[pl.ds(d, 3)].reshape(3 * I, PLANE)
        right_low = gl[pl.ds(d, 3)].reshape(3 * I, PLANE)
        taps[...] = product(w9h[...], w9l[...], right_high, right_low, ((1,), (0,)))

        def line(b):
            def tap(c):
                k = 3 * b + c
                return taps[k * O : (k + 1) * O, :]

            total = tap(1)
            total += jnp.where(not_left, pltpu.roll(tap(0), 1, 1), 0.0)
            total += jnp.where(not_right, pltpu.roll(tap(2), PLANE - 1, 1), 0.0)
            return total

        total = line(1)
        total += jnp.where(not_top, pltpu.roll(line(0), WIDTH, 1), 0.0)
        total += jnp.where(not_bottom, pltpu.roll(line(2), PLANE - WIDTH, 1), 0.0)
        part[d] = total
        return carry

    rs_sems = (rs_s, rs_r)
    reduce = []

    def reduce_start(n):
        d, w = REDUCE_CHUNKS[n]
        planes = pl.ds(d, w)
        reduce.append(
            [
                push(
                    part.at[planes, rows(x_of(j)), :], prec.at[j - 1, planes],
                    rs_sems, (n, j - 1), at_x(j),
                )
                for j in (2, 1, 3)
            ]
        )

    ag_sems = (ag_s, ag_r)
    spread = []

    def activate(n):
        d, w = REDUCE_CHUNKS[n]
        for copy in reduce[n]:
            copy.wait_recv()
        for e in range(d, d + w):
            total = part[e, rows(x), :] + prec[0, e] + (prec[1, e] + prec[2, e])
            positive = jnp.maximum(total, 0.0)
            actv[:, e, :] = positive * positive
            pgx[1 + e, rows(x), :] = 2.0 * positive * ogv[:, e, :]
        here = pgx.at[pl.ds(1 + d, w), rows(x), :]
        spread.append([push(here, here, ag_sems, (n, j - 1), at_x(j)) for j in (2, 1, 3)])

    for n, (d, w) in enumerate(REDUCE_CHUNKS):
        if n == 2:
            edge_arrive()
            halve(0, 0)
            halve(PLANES + 1, 0)
        lax.fori_loop(d, d + w, forward, 0)
        reduce_start(n)
        if n == 1:
            bring_og.wait()
        if n > 1:
            activate(n - 2)
    lax.fori_loop(0, wc.shape[0] // 128, transpose, 0)
    activate(2)
    activate(3)
    give_act = pltpu.make_async_copy(actv, act, local.at[0])
    give_act.start()

    def stack(e, carry):
        field = pgx[e]
        for b in range(3):
            if b == 0:
                moved = jnp.where(not_bottom, pltpu.roll(field, PLANE - WIDTH, 1), 0.0)
            elif b == 1:
                moved = field
            else:
                moved = jnp.where(not_top, pltpu.roll(field, WIDTH, 1), 0.0)
            for c in range(3):
                if c == 0:
                    last = jnp.where(not_right, pltpu.roll(moved, PLANE - 1, 1), 0.0)
                elif c == 1:
                    last = moved
                else:
                    last = jnp.where(not_left, pltpu.roll(moved, 1, 1), 0.0)
                k = 3 * b + c
                high, low = split(last)
                sh[e, k * O : (k + 1) * O, :] = high
                sl[e, k * O : (k + 1) * O, :] = low
        return carry

    def weigh(d, w):
        lax.fori_loop(d + 1, d + 1 + w, stack, 0)

        def fields(stacked):
            return jnp.concatenate([stacked[e] for e in range(d + 1, d + 1 + w)], axis=1)

        def inputs(held):
            return jnp.concatenate(
                [held[e : e + 3].reshape(3 * I, PLANE) for e in range(d, d + w)], axis=1
            )

        wacc[...] += product(fields(sh), fields(sl), inputs(gh), inputs(gl), ((1,), (1,)))

    rim_start, rim_arrive, rim_leave = neighbours(pgx, ph_s, ph_r)
    for n, (d, w) in enumerate(REDUCE_CHUNKS):
        for copy in spread[n]:
            copy.wait_recv()
        if n == 3:
            rim_start()
            leaves.append(rim_leave)
        weigh(d, w)

    for a in range(3):
        for k in range(9):
            block = wacc[k * O : (k + 1) * O, a * I : (a + 1) * I]
            wsum[:, 9 * a + k] = block.reshape(X, ROWS, I)

    near = core * H
    first = push(
        wsum.at[:, pl.ds((1 - core) * H, H)], w1b, (w1_s, w1_r), 0, (mate, f)
    )

    def backward(d, carry):
        high = jnp.dot(
            wt[:, : TAPS * O], sh[pl.ds(d, 3)].reshape(TAPS * O, PLANE),
            preferred_element_type=F32,
        )
        low = jnp.dot(
            wt[:I, : TAPS * O], sl[pl.ds(d, 3)].reshape(TAPS * O, PLANE),
            preferred_element_type=F32,
        )
        value = high[:I] + (high[I:] + low)
        igp[d] = value.reshape(GY, GZ * ROWS, PLANE)
        return carry

    in_sems = (in_s, in_r)
    inward = []

    def input_start(n):
        d, w, way = INPUT_CHUNKS[n]
        planes = pl.ds(d, w)
        lax.fori_loop(d, d + w, backward, 0)
        inward.append(
            {
                "far": push(
                    igp.at[planes, :, rows(z_of(2)), :], zrel.at[planes],
                    in_sems, (n, 0), at_z(way),
                ),
                "back": push(
                    igp.at[planes, :, rows(z_of(-way)), :], zrec.at[1, planes],
                    in_sems, (n, 1), at_z(-way),
                ),
            }
        )

    def input_relay(n):
        d, w, way = INPUT_CHUNKS[n]
        planes = pl.ds(d, w)
        inward[n]["far"].wait_recv()
        igp[planes, :, rows(z_of(way)), :] += zrel[planes]
        inward[n]["on"] = push(
            igp.at[planes, :, rows(z_of(way)), :], zrec.at[0, planes],
            in_sems, (n, 2), at_z(way),
        )

    def input_pair(n):
        d, w, way = INPUT_CHUNKS[n]
        planes = pl.ds(d, w)
        inward[n]["back"].wait_recv()
        inward[n]["on"].wait_recv()
        igp[planes, :, rows(gz), :] += zrec[0, planes] + zrec[1, planes]
        inward[n]["y"] = push(
            igp.at[planes, 1 - gy, rows(gz), :], yrec.at[planes], in_sems, (n, 3), at_y
        )

    def input_end(n):
        d, w, way = INPUT_CHUNKS[n]
        inward[n]["y"].wait_recv()
        for e in range(d, d + w):
            igv[:, e, :] = igp[e, gy, rows(gz), :] + yrec[e]

    wy_sems = (wy_s, wy_r)
    wx_sems = (wx_s, wx_r)
    weights = []

    def weight_start(n):
        t, w = TAP_CHUNKS[n]
        part_of = pl.ds(near + t, w)
        wsum[:, part_of] += w1b[:, t : t + w]
        weights.append(
            {
                "y": push(
                    wsum.at[:, part_of], warr.at[:, pl.ds(t, w)], wy_sems, n, (across, f)
                )
            }
        )

    scale = 1.0 / math.sqrt(PLANES * SLABS * PLANE)

    def weight_sum(n):
        t, w = TAP_CHUNKS[n]
        part_of = pl.ds(near + t, w)
        weights[n]["y"].wait_recv()
        wtot[:, t : t + w] = (wsum[:, part_of] + warr[:, t : t + w]) * scale
        for j in (2, 1, 3):
            weights[n]["x", j] = push(
                wtot.at[x_of(j), pl.ds(t, w)], wout.at[part_of, :, lanes(x)],
                wx_sems, (n, j - 1), at_x(j),
            )
        wout[part_of, :, lanes(x)] = wtot[x, t : t + w]

    def weight_swap(n):
        t, w = TAP_CHUNKS[n]
        for j in (1, 2, 3):
            weights[n]["x", j].wait_recv()
        here = wout.at[pl.ds(near + t, w)]
        weights[n]["mate"] = push(here, here, (w5_s, w5_r), n, (mate, f))

    input_start(0)
    first.wait_recv()
    for n in (0, 1, 2, 3):
        weight_start(n)
    input_start(1)
    rim_arrive()
    stack(0, 0)
    stack(PLANES + 1, 0)
    input_relay(0)
    input_start(2)
    input_relay(1)
    input_start(3)
    input_relay(2)
    weight_sum(0)
    weight_sum(1)
    input_pair(0)
    input_relay(3)
    input_pair(1)
    weight_sum(2)
    weight_sum(3)
    input_pair(2)
    weight_swap(0)
    weight_swap(1)
    input_end(0)
    input_end(1)
    input_pair(3)
    input_end(2)
    weight_swap(2)
    weight_swap(3)
    input_end(3)
    give_ig = pltpu.make_async_copy(igv, ig, local.at[1])
    give_ig.start()
    gifts = [give_act, give_ig]
    for n, (t, w) in enumerate(TAP_CHUNKS):
        weights[n]["mate"].wait_recv()
        for k in range(2):
            taps_of = pl.ds(k * H + t, min(w, TAPS - k * H - t))
            give = pltpu.make_async_copy(wout.at[taps_of], wg.at[taps_of], local.at[2 + 2 * n + k])
            give.start()
            gifts.append(give)

    for copy in sent:
        copy.wait_send()
    edge_leave()
    rim_leave()
    for give in gifts:
        give.wait()


def scratch():
    I = ROWS * G
    O = ROWS * X
    H = PAD // 2
    columns = -(-TAPS * O // 128) * 128
    vmem = pltpu.VMEM
    dma = pltpu.SemaphoreType.DMA
    return [
        vmem((ROWS, PLANES, PLANE), F32),
        vmem((ROWS, PLANES, PLANE), F32),
        vmem((ROWS, PLANES, PLANE), F32),
        vmem((ROWS, PLANES, PLANE), F32),
        vmem((PLANES + 2, GY, GZ * ROWS, PLANE), F32),
        vmem((PLANES + 2, I, PLANE), BF16),
        vmem((PLANES + 2, I, PLANE), BF16),
        vmem((X, TAPS, ROWS, I), F32),
        vmem((9 * O, 3 * I), BF16),
        vmem((9 * O, 3 * I), BF16),
        vmem((columns, I), F32),
        vmem((2 * I, columns), BF16),
        vmem((9 * O, PLANE), F32),
        vmem((PLANES, O, PLANE), F32),
        vmem((X - 1, PLANES, ROWS, PLANE), F32),
        vmem((PLANES + 2, O, PLANE), F32),
        vmem((PLANES + 2, 9 * O, PLANE), BF16),
        vmem((PLANES + 2, 9 * O, PLANE), BF16),
        vmem((9 * O, 3 * I), F32),
        vmem((X, PAD, ROWS, I), F32),
        vmem((X, H, ROWS, I), F32),
        vmem((X, H, ROWS, I), F32),
        vmem((X, H, ROWS, I), F32),
        vmem((PAD, ROWS, X * I), F32),
        vmem((PLANES, GY, GZ * ROWS, PLANE), F32),
        vmem((PLANES, GY, ROWS, PLANE), F32),
        vmem((2, PLANES, GY, ROWS, PLANE), F32),
        vmem((PLANES, ROWS, PLANE), F32),
        dma((10,)),
        dma((len(GATHER_CHUNKS), 6)), dma((len(GATHER_CHUNKS), 6)),
        dma((6,)), dma((6,)),
        dma((2,)), dma((2,)),
        dma((4, 3)), dma((4, 3)),
        dma((4, 3)), dma((4, 3)),
        dma((2,)), dma((2,)),
        dma((4, 4)), dma((4, 4)),
        dma((1,)), dma((1,)),
        dma((4,)), dma((4,)),
        dma((4, 3)), dma((4, 3)),
        dma((4,)), dma((4,)),
    ]


def hand_out(act, ig, wg, act_out, ig_out, wg_out, act_held, ig_held, wg_held, into, out):
    parts = [(act, act_held, act_out), (ig, ig_held, ig_out)]
    third = TAPS // 3
    for n in range(3):
        part = pl.ds(n * third, third)
        parts.append((wg.at[part], wg_held.at[part], wg_out.at[part]))
    bring = [pltpu.make_async_copy(p[0], p[1], into.at[n]) for n, p in enumerate(parts)]
    give = [pltpu.make_async_copy(p[1], p[2], out.at[n]) for n, p in enumerate(parts)]
    for copy in bring:
        copy.start()
    for first, second in zip(bring, give):
        first.wait()
        second.start()
    for copy in give:
        copy.wait()


def shards(volume, filters, out_grad):
    anywhere = pl.BlockSpec(memory_space=pl.ANY)
    shapes = (
        jax.ShapeDtypeStruct(volume.shape, F32),
        jax.ShapeDtypeStruct(volume.shape, F32),
        jax.ShapeDtypeStruct(filters.shape, F32),
    )
    held = pl.pallas_call(
        kernel,
        out_shape=shapes,
        in_specs=[anywhere] * 3,
        out_specs=(anywhere,) * 3,
        scratch_shapes=scratch(),
        compiler_params=pltpu.CompilerParams(
            collective_id=0, has_side_effects=True, vmem_limit_bytes=56 * 2**20
        ),
    )(volume, filters, out_grad)
    return pl.pallas_call(
        hand_out,
        out_shape=shapes,
        in_specs=[anywhere] * 3,
        out_specs=(anywhere,) * 3,
        scratch_shapes=[
            *(pltpu.VMEM(shape.shape, F32) for shape in shapes),
            pltpu.SemaphoreType.DMA((5,)), pltpu.SemaphoreType.DMA((5,)),
        ],
    )(*held)


def solution(mesh):
    placed = (P("filt", "slab", None), P(None, "filt", None), P("filt", "slab", None))
    return jax.shard_map(
        shards,
        mesh=mesh,
        in_specs=placed,
        out_specs=(P("filt", "slab", None), P("filt", "slab", None), P(None, "filt", None)),
        check_vma=False,
    )
```
